512 devices in a mesh: dp: 4 (over y_hi, core), rep: 4 (over x), blk: 32 (over z, y_lo).
Axes of the slice: x: 4, y: 4 (y_hi: 2, y_lo: 2; y = y_hi * 2 + y_lo), z: 16, core: 2. Of those that a mesh axis runs over, the one named last changes fastest.
Arguments:
- features: bfloat16 [32768, 512], P(('dp', 'blk')), parts along dimension 0, may hold values from -6 to 6
- pre_act: bfloat16 [32768, 512], P(('dp', 'blk')), parts along dimension 0, may hold values from -6 to 6
- upstream: bfloat16 [32768, 512], P(('dp', 'blk')), parts along dimension 0, may hold values from -6 to 6
- weight: bfloat16 [512, 512], replicated, may hold values from -0.25 to 0.25
- tile_values: bfloat16 [128, 32, 6, 128, 128], P(('dp', 'blk'), 'rep'), parts along dimension 0, may hold values from -0.09375 to 0.09375
- tile_rows: int32 [128, 32, 6], P(('dp', 'blk'), 'rep'), parts along dimension 0, may hold values from 0 to 1
- tile_cols: int32 [128, 32, 6], P(('dp', 'blk'), 'rep'), parts along dimension 0, may hold values from 0 to 1
- tile_count: int32 [128, 32], P(('dp', 'blk'), 'rep'), parts along dimension 0, may hold values from 0 to 6, as said below
Outputs:
- grad_feat: bfloat16 [32768, 512], P(('dp', 'blk')), parts along dimension 0
- grad_weight: float32 [2048, 512], P(('dp', 'blk')), parts along dimension 0
The draws below stay inside these ranges and needn't reach their ends.
There are 4 independent parts, one for each index of `dp`. The reference program is written for one: setup_inputs(seed, part) draws one part's arguments, and reference() takes and returns one part's arrays. A program takes and returns all parts, laid end to end along the dimension named above; an argument that names none is the same for every part. Nothing has to cross between parts.
Inputs may be any that keep to these rules, and one draw needn't show every extreme that they name: `tile_rows`: local tile row block of the cycle position. `tile_cols`: local tile column block of the column owner. The first tile_count[b,k] slots of step k are live and the rest are ignored; every cycle position has a step with all 6 slots live.
All inputs are finite; a program needn't handle non-finite values.
Results may differ from the reference program's by a relative error of at most 0.0049.
Values may be sent and summed in bfloat16 or wider, within the bound.
No kernel may reach another device: no remote copies, remote signals or barrier semaphores. Data moves between devices by JAX's collectives and lax.ppermute only.
A program may use at most 64 MiB of HBM per device.

```python
import jax
import jax.numpy as jnp
from jax import lax

F = 512
H = 512
TILE = 128
ROW_BLOCKS = 2
CAP = 6
CYCLE = 32
STEPS = 32
NODES = 8192


def draw_tile_count(key, part):
    key = jax.random.fold_in(key, 11)
    first_key, second_key, third_key = jax.random.split(key, 3)
    lower_draw = jax.random.randint(first_key, (CYCLE, STEPS), 0, CAP + 1)
    upper_draw = jax.random.randint(second_key, (CYCLE, STEPS), 0, CAP + 1)
    chosen = jax.random.randint(third_key, (CYCLE, 1), 0, STEPS)
    filled = jnp.arange(STEPS, dtype=jnp.int32)[None, :] == chosen
    return jnp.where(filled, CAP, jnp.minimum(lower_draw, upper_draw)).astype(jnp.int32)


def touch_ends(array, own_key, least, largest):
    longest = array.shape.index(max(array.shape))
    spots = []
    for shift in (0, 1):
        where = [jax.random.randint(jax.random.fold_in(own_key, axis), (), 0, length) for axis, length in enumerate(array.shape)]
        where[longest] = (where[longest] + shift) % array.shape[longest]
        spots.append(tuple(where))
    return array.at[spots[0]].set(least).at[spots[1]].set(largest)


def spiked(result, rng, source, target, parts, factor):
    owner, partner = [(jnp.arange(result.shape[dim]) // (result.shape[dim] // parts)).reshape([-1 if axis == dim else 1 for axis in range(result.ndim)]) for dim in (source, target)]
    chosen = jax.random.permutation(rng, parts)[partner]
    strong = (owner == chosen) | (owner == (partner + parts // 2) % parts)
    return jnp.where(strong, factor * result, result)


def block_scale(rng, dims, pieces, low, high):
    loudness = 1.0
    for position, shards_of in pieces:
        heights = jax.random.uniform(jax.random.fold_in(jax.random.fold_in(rng, 6), position), (shards_of,), jnp.float32, low / len(pieces), high / len(pieces))
        loudness = loudness * jnp.repeat(jnp.exp(heights), dims[position] // shards_of).reshape((-1,) + (1,) * (len(dims) - 1 - position))
    return loudness


def centred(key, extent, deviation, bound, cuts=(), kind=jnp.bfloat16):
    factor_of = block_scale(key, extent, cuts, -0.22, 0.18) if cuts else 1.0
    drawn = jax.random.normal(key, extent, jnp.float32) * deviation * factor_of
    return jnp.minimum(jnp.maximum(drawn, -bound), bound).astype(kind)


def bell_draw_with(own_key, shape, deviation, limit, cuts, heavy, kind=jnp.bfloat16):
    drawn = deviation * jax.random.normal(own_key, shape, jnp.float32)
    if cuts:
        drawn = drawn * block_scale(own_key, shape, cuts, -0.22, 0.18)
    return jnp.clip(spiked(drawn, jax.random.fold_in(own_key, 3), *heavy), -limit, limit).astype(kind)


def setup_inputs(seed: int = 0, part: int = 0) -> dict:
    key_list = jax.random.split(jax.random.key(seed), 9)
    own_keys = jax.random.split(jax.random.fold_in(key_list[8], part), 9)
    features = centred(own_keys[0], (NODES, F), 1.0, 6.0, ((0, 32),))
    pre_act = centred(own_keys[1], (NODES, H), 1.0, 6.0, ((0, 32),))
    upstream = bell_draw_with(own_keys[2], (NODES, H), 1.0, 6.0, ((0, 32),), (0, 1, 32, 2.75))
    weight = centred(key_list[3], (H, F), H ** -0.5, 0.25)
    tile_values = centred(own_keys[4], (CYCLE, STEPS, CAP, TILE, TILE), (TILE * max(STEPS * CAP // (3 * ROW_BLOCKS), 1)) ** -0.5, 0.09375, ((0, 32), (1, 4)))
    tile_rows = touch_ends(jax.random.randint(own_keys[5], (CYCLE, STEPS, CAP), 0, ROW_BLOCKS), jax.random.fold_in(own_keys[5], 1), 0, ROW_BLOCKS - 1).astype(jnp.int32)
    tile_cols = touch_ends(jax.random.randint(own_keys[6], (CYCLE, STEPS, CAP), 0, ROW_BLOCKS), jax.random.fold_in(own_keys[6], 1), 0, ROW_BLOCKS - 1).astype(jnp.int32)
    tile_count = draw_tile_count(jax.random.fold_in(jax.random.fold_in(key_list[8], part), 71), part)
    return dict(features=features, pre_act=pre_act, upstream=upstream, weight=weight, tile_values=tile_values, tile_rows=tile_rows, tile_cols=tile_cols, tile_count=tile_count)


def reference(features, pre_act, upstream, weight, tile_values, tile_rows, tile_cols, tile_count):
    node_count, feat_width = features.shape
    cycle_size = tile_values.shape[0]
    step_count = tile_values.shape[1]
    slot_count = tile_values.shape[2]
    tile_size = tile_values.shape[3]
    blocks = node_count // (cycle_size * tile_size)
    source = features.reshape(cycle_size * blocks, tile_size, feat_width)
    grad_out = jnp.where(pre_act > 0, upstream, jnp.zeros_like(upstream))
    back_grad = jnp.dot(grad_out, weight, preferred_element_type=jnp.float32).astype(jnp.bfloat16)
    back_blocks = back_grad.reshape(cycle_size * blocks, tile_size, feat_width)

    def visit(totals, flat_index):
        aggregate, feat_grad = totals
        row_owner = flat_index // step_count
        step_index = flat_index % step_count
        col_owner = (row_owner - step_index) % cycle_size
        tile_vals = tile_values[row_owner, step_index]
        row_index = (row_owner * blocks + tile_rows[row_owner, step_index]).astype(jnp.int32)
        col_index = (col_owner * blocks + tile_cols[row_owner, step_index]).astype(jnp.int32)
        live_count = tile_count[row_owner, step_index]
        for slot_index in range(slot_count):
            matrix = tile_vals[slot_index]
            live_flag = slot_index < live_count
            forward = jnp.dot(matrix, source[col_index[slot_index]], preferred_element_type=jnp.float32)
            aggregate = aggregate.at[row_index[slot_index]].add(jnp.where(live_flag, forward, jnp.zeros_like(forward)))
            backward = lax.dot_general(matrix, back_blocks[row_index[slot_index]], (((0,), (0,)), ((), ())), preferred_element_type=jnp.float32)
            feat_grad = feat_grad.at[col_index[slot_index]].add(jnp.where(live_flag, backward, jnp.zeros_like(backward)))
        return (aggregate, feat_grad), None

    zeros = jnp.zeros((cycle_size * blocks, tile_size, feat_width), jnp.float32)
    (aggregate, feat_grad), unused = lax.scan(visit, (zeros, zeros), jnp.arange(cycle_size * step_count, dtype=jnp.int32))
    aggregate_low = aggregate.reshape(node_count, feat_width).astype(jnp.bfloat16)
    loss_scale = node_count ** -0.5
    grad_weight = lax.dot_general(grad_out, aggregate_low, (((0,), (0,)), ((), ())), preferred_element_type=jnp.float32) * loss_scale
    grad_feat = feat_grad.reshape(node_count, feat_width).astype(jnp.bfloat16)
    return (grad_feat, grad_weight)
```

```python
import functools

import jax
import jax.numpy as jnp
import numpy as np
from jax import lax
from jax.experimental import pallas as pl
from jax.experimental.pallas import tpu as pltpu
from jax.sharding import Mesh, PartitionSpec as P

ZH, ZL, YL, REP = 4, 4, 2, 4
BLK = ("zh", "zl", "yl")
BF16, F32 = jnp.bfloat16, jnp.float32
VMEM_LIMIT = 48 * 1024 * 1024


def contract_rows(left, right):
    return lax.dot_general(left, right, (((0,), (0,)), ((), ())), preferred_element_type=F32)


def hidden_order(width):
    rows = width // (ZH * ZL * YL)
    units = np.arange(width).reshape(ZH, ZL, YL, REP, rows // REP)
    return units.transpose(3, 1, 2, 0, 4).reshape(-1)


def dense_kernel(rows_ref, cols_ref, count_ref, tiles_ref, out_ref, acc_ref, *, odd):
    step = 2 * pl.program_id(0) + odd
    slots, tile = tiles_ref.shape[2], tiles_ref.shape[3]
    acc_ref[...] = jnp.zeros_like(acc_ref)
    live = count_ref[step]
    for q in range(slots):

        @pl.when(q < live)
        def _():
            row, col = rows_ref[step * slots + q], cols_ref[step * slots + q]
            acc_ref[row, col] += tiles_ref[0, 0, q].astype(F32)

    for row in range(2):
        for col in range(2):
            out_ref[row * tile : (row + 1) * tile, col * tile : (col + 1) * tile] = acc_ref[
                row, col
            ].astype(BF16)


def dense_steps(tiles, rows, cols, count, odd):
    pairs, _, slots, tile, _ = tiles.shape
    return pl.pallas_call(
        functools.partial(dense_kernel, odd=odd),
        grid_spec=pltpu.PrefetchScalarGridSpec(
            num_scalar_prefetch=3,
            grid=(pairs,),
            in_specs=[pl.BlockSpec((1, 1, slots, tile, tile), lambda i, *_: (i, odd, 0, 0, 0))],
            out_specs=pl.BlockSpec((2 * tile, 2 * tile), lambda i, *_: (0, i)),
            scratch_shapes=[pltpu.VMEM((2, 2, tile, tile), F32)],
        ),
        out_shape=jax.ShapeDtypeStruct((2 * tile, pairs * 2 * tile), BF16),
        cost_estimate=pl.CostEstimate(flops=0, bytes_accessed=2 * tiles.size, transcendentals=0),
    )(rows, cols, count, tiles)


def partial_kernel(zl_ref, even_ref, odd_ref, own_ref, next_ref, out_ref):
    rows, wide = even_ref.shape
    quarter = out_ref.shape[3]
    for m in range(wide // rows):
        span = slice(m * rows, (m + 1) * rows)
        block = contract_rows(even_ref[:, span], own_ref[...])
        block += contract_rows(odd_ref[:, span], next_ref[...])
        block = block.astype(BF16)
        slot = lax.rem(zl_ref[0] + ZL - m, ZL)
        for q in range(REP):
            out_ref[q, slot] = block[:, q * quarter : (q + 1) * quarter]


def gather_kernel(zh_ref, zl_ref, in_ref, out_ref):
    zh, zl = zh_ref[0], zl_ref[0]
    for d in range(ZH):
        total = jnp.zeros(out_ref.shape[1:], F32)
        for s in range(ZL):
            borrow = (s < zl).astype(jnp.int32)
            total += in_ref[lax.rem(zh - d - borrow + 2 * ZH, ZH), s].astype(F32)
        out_ref[d] = total.astype(BF16)


def weight_kernel(in_ref, feat_ref, p_ref, gw_ref, *, scale):
    total = in_ref[0].astype(F32)
    for d in range(1, in_ref.shape[0]):
        total += in_ref[d].astype(F32)
    p_ref[...] = total.astype(BF16)
    gw_ref[...] = (contract_rows(p_ref[...], feat_ref[...]) * scale).astype(BF16)


def feature_kernel(p_ref, weight_ref, out_ref):
    quarter = p_ref.shape[2]
    rows = out_ref.shape[0]
    total = jnp.zeros(out_ref.shape, F32)
    for q in range(p_ref.shape[0]):
        total += jnp.dot(
            p_ref[q, :rows, :],
            weight_ref[q * quarter : (q + 1) * quarter, :],
            preferred_element_type=F32,
        )
    out_ref[...] = total.astype(BF16)


def whole(kernel, outs, scalars, arrays):
    return pl.pallas_call(
        kernel,
        in_specs=[pl.BlockSpec(memory_space=pltpu.SMEM)] * len(scalars)
        + [pl.BlockSpec(memory_space=pltpu.VMEM)] * len(arrays),
        out_specs=jax.tree.map(lambda _: pl.BlockSpec(memory_space=pltpu.VMEM), outs),
        out_shape=outs,
        compiler_params=pltpu.CompilerParams(vmem_limit_bytes=VMEM_LIMIT),
    )(*scalars, *arrays)


def exchange(value, axes):
    return lax.all_to_all(value, axes, 0, 0)


def to_previous(value):
    count = ZH * ZL * YL
    return lax.ppermute(value, BLK, [(b, (b - 1) % count) for b in range(count)])


def shards(features, pre_act, upstream, weight, tile_values, tile_rows, tile_cols, tile_count):
    _, steps, slots, tile, _ = tile_values.shape
    nodes, width = features.shape
    hidden = upstream.shape[1]
    quarter = hidden // REP
    scale = float(nodes * ZH * ZL * YL) ** -0.5
    zh = lax.axis_index("zh").reshape(1)
    zl = lax.axis_index("zl").reshape(1)
    shape = jax.ShapeDtypeStruct

    spread = np.zeros((hidden, hidden), np.float32)
    spread[hidden_order(hidden), np.arange(hidden)] = 1.0
    spread = jnp.asarray(spread, BF16)
    grad_out = jnp.where(pre_act > 0, upstream, jnp.zeros_like(upstream))
    own = jnp.dot(grad_out, spread, preferred_element_type=F32).astype(BF16)
    weight = contract_rows(spread, weight).astype(BF16)

    tiles = tile_values.reshape(steps // 2, 2, slots, tile, tile)
    places = (tile_rows.reshape(-1), tile_cols.reshape(-1), tile_count.reshape(-1))
    following = to_previous(own)
    odd = to_previous(dense_steps(tiles, *places, 1))
    even = dense_steps(tiles, *places, 0)

    parts = whole(
        partial_kernel, shape((REP, ZL, nodes, quarter), BF16), (zl,), (even, odd, own, following)
    )
    parts = exchange(parts.reshape(REP * ZL, nodes, quarter), ("rep", "zl"))
    parts = whole(
        gather_kernel,
        shape((ZH, nodes, quarter), BF16),
        (zh, zl),
        (parts.reshape(REP, ZL, nodes, quarter),),
    )
    parts = exchange(parts, "zh")
    p_quarter, gw = whole(
        functools.partial(weight_kernel, scale=scale),
        (shape((nodes, quarter), BF16), shape((quarter, width), BF16)),
        (),
        (parts, features),
    )
    lanes = ZL * YL
    gw = exchange(gw.reshape(lanes, quarter // lanes, width), ("zl", "yl"))
    gw = jnp.sum(gw.astype(F32), axis=0).astype(BF16)
    gw = exchange(gw.reshape(ZH, quarter // (lanes * ZH), width), "zh")
    gw = jnp.sum(gw.astype(F32), axis=0)
    high = lax.reduce_precision(gw, 8, 7)
    gw_rows = gw.size // quarter
    packed = jnp.concatenate(
        [
            p_quarter,
            high.astype(BF16).reshape(gw_rows, quarter),
            (gw - high).astype(BF16).reshape(gw_rows, quarter),
        ]
    )
    packed = exchange(jnp.broadcast_to(packed[None], (REP,) + packed.shape), "rep")
    grad_feat = whole(feature_kernel, shape((nodes, width), BF16), (), (packed, weight))
    high = packed[:, nodes : nodes + gw_rows].astype(F32)
    low = packed[:, nodes + gw_rows :].astype(F32)
    return grad_feat, (high + low).reshape(-1, width)


def solution(mesh):
    dp = mesh.shape["dp"]
    fine = Mesh(mesh.devices.reshape(dp, REP, ZH, ZL, YL), ("dp", "rep") + BLK)
    rows = ("dp",) + BLK
    return jax.shard_map(
        shards,
        mesh=fine,
        in_specs=(
            P(rows, None),
            P(rows, None),
            P(rows, None),
            P(),
            P(rows, "rep", None, None, None),
            P(rows, "rep", None),
            P(rows, "rep", None),
            P(rows, "rep"),
        ),
        out_specs=(P(rows, None), P(rows, None)),
        check_vma=False,
    )
```

```python
import functools

import jax
import jax.numpy as jnp
import numpy as np
from jax import lax
from jax.experimental import pallas as pl
from jax.experimental.pallas import tpu as pltpu
from jax.sharding import Mesh, PartitionSpec as P

ZH, ZL, YL, REP = 4, 4, 2, 4
BLK = ("zh", "zl", "yl")
BF16, F32 = jnp.bfloat16, jnp.float32
VMEM_LIMIT = 48 * 1024 * 1024


def contract_rows(left, right):
    return lax.dot_general(left, right, (((0,), (0,)), ((), ())), preferred_element_type=F32)


def hidden_order(width):
    units = np.arange(width).reshape(ZH * ZL * YL, REP, -1)
    return units.transpose(1, 0, 2).reshape(-1)


def dense_kernel(rows_ref, cols_ref, count_ref, tiles_ref, out_ref, acc_ref, *, places):
    slots, tile = tiles_ref.shape[2], tiles_ref.shape[3]
    for at, step in enumerate(places):
        acc_ref[...] = jnp.zeros_like(acc_ref)
        live = count_ref[0, step]
        for q in range(slots):

            @pl.when(q < live)
            def _():
                row, col = rows_ref[q, 0, step], cols_ref[q, 0, step]
                acc_ref[row, col] += tiles_ref[0, step, q].astype(F32)

        for row in range(2):
            for col in range(2):
                left = (2 * at + col) * tile
                out_ref[row * tile : (row + 1) * tile, left : left + tile] = acc_ref[
                    row, col
                ].astype(BF16)


def partial_kernel(even_ref, odd_ref, own_ref, next_ref, *out_refs, first):
    rows = even_ref.shape[0]
    for m, out_ref in enumerate(out_refs):
        span = slice(m * rows, (m + 1) * rows)
        far = slice((first + m) * rows, (first + m + 1) * rows)
        block = contract_rows(even_ref[:, far], own_ref[...])
        block += contract_rows(odd_ref[:, span], next_ref[...])
        out_ref[...] = block.astype(out_ref.dtype)


def near_kernel(keep_ref, first_ref, second_ref, third_ref, out_ref):
    quarter = out_ref.shape[2]
    for q in range(out_ref.shape[0]):
        span = slice(q * quarter, (q + 1) * quarter)
        total = keep_ref[:, span] + first_ref[:, span].astype(F32)
        total += second_ref[:, span].astype(F32) + third_ref[:, span].astype(F32)
        out_ref[q] = total.astype(BF16)


def weight_kernel(*refs, scale):
    *in_refs, feat_ref, p_ref, gw_ref = refs
    total = in_refs[0][...].astype(F32)
    for in_ref in in_refs[1:]:
        total += in_ref[...].astype(F32)
    p_ref[...] = total.astype(BF16)
    gw_ref[...] = (contract_rows(p_ref[...], feat_ref[...]) * scale).astype(BF16)


def feature_kernel(p_ref, weight_ref, out_ref):
    quarter = p_ref.shape[2]
    rows = out_ref.shape[0]
    total = jnp.zeros(out_ref.shape, F32)
    for q in range(p_ref.shape[0]):
        total += jnp.dot(
            p_ref[q, :rows, :],
            weight_ref[q * quarter : (q + 1) * quarter, :],
            preferred_element_type=F32,
        )
    out_ref[...] = total.astype(BF16)


def whole(kernel, outs, scalars, arrays, scratch=()):
    return pl.pallas_call(
        kernel,
        in_specs=[pl.BlockSpec(memory_space=pltpu.SMEM)] * len(scalars)
        + [pl.BlockSpec(memory_space=pltpu.VMEM)] * len(arrays),
        out_specs=jax.tree.map(lambda _: pl.BlockSpec(memory_space=pltpu.VMEM), outs),
        out_shape=outs,
        scratch_shapes=scratch,
        compiler_params=pltpu.CompilerParams(vmem_limit_bytes=VMEM_LIMIT),
    )(*scalars, *arrays)


def exchange(value, axes):
    return lax.all_to_all(value, axes, 0, 0)


def move(value, axes, count, shift):
    return lax.ppermute(value, axes, [(i, (i + shift) % count) for i in range(count)])


def shards(features, pre_act, upstream, weight, tile_values, tile_rows, tile_cols, tile_count):
    _, steps, slots, tile, _ = tile_values.shape
    nodes, width = features.shape
    hidden = upstream.shape[1]
    quarter = hidden // REP
    scale = float(nodes * ZH * ZL * YL) ** -0.5
    ring = functools.partial(move, axes=BLK, count=ZH * ZL * YL)
    column = functools.partial(move, axes=("zh", "zl"), count=ZH * ZL)
    shape = jax.ShapeDtypeStruct

    spread = np.zeros((hidden, hidden), np.float32)
    spread[hidden_order(hidden), np.arange(hidden)] = 1.0
    spread = jnp.asarray(spread, BF16)
    grad_out = jnp.where(pre_act > 0, upstream, jnp.zeros_like(upstream))
    own = jnp.dot(grad_out, spread, preferred_element_type=F32).astype(BF16)
    weight = contract_rows(spread, weight).astype(BF16)

    def dense(places):
        return whole(
            functools.partial(dense_kernel, places=places),
            shape((2 * tile, len(places) * 2 * tile), BF16),
            (tile_rows.transpose(2, 0, 1), tile_cols.transpose(2, 0, 1), tile_count),
            (tile_values,),
            (pltpu.VMEM((2, 2, tile, tile), F32),),
        )

    following = ring(own, shift=-1)
    odd_high = ring(dense((5, 7)), shift=-1)
    odd_low = ring(dense((1, 3)), shift=-1)
    even = dense((0, 2, 4, 6))
    block = shape((nodes, hidden), BF16)
    second, third = whole(
        functools.partial(partial_kernel, first=2),
        (block, block),
        (),
        (even, odd_high, own, following),
    )
    third = column(third, shift=-2)
    second = column(second, shift=-1)
    zeroth, keep = whole(
        functools.partial(partial_kernel, first=0),
        (block, shape((nodes, hidden), F32)),
        (),
        (even, odd_low, own, following),
    )
    zeroth = column(zeroth, shift=1)
    parts = whole(
        near_kernel,
        shape((REP, nodes, quarter), BF16),
        (),
        (keep, third, second, zeroth),
    )
    parts = exchange(parts, "rep")
    parts = [column(parts[r], shift=-1 - ZL * r) for r in (2, 1, 3, 0)]
    p_quarter, gw = whole(
        functools.partial(weight_kernel, scale=scale),
        (shape((nodes, quarter), BF16), shape((quarter, width), BF16)),
        (),
        (*parts, features),
    )
    gw = exchange(gw.reshape(ZH * ZL * YL, -1, width), BLK)
    gw = jnp.sum(gw.astype(F32), axis=0)
    high = lax.reduce_precision(gw, 8, 7)
    gw_rows = gw.size // quarter
    packed = jnp.concatenate(
        [
            p_quarter,
            high.astype(BF16).reshape(gw_rows, quarter),
            (gw - high).astype(BF16).reshape(gw_rows, quarter),
        ]
    )
    packed = exchange(jnp.broadcast_to(packed[None], (REP,) + packed.shape), "rep")
    grad_feat = whole(feature_kernel, shape((nodes, width), BF16), (), (packed, weight))
    high = packed[:, nodes : nodes + gw_rows].astype(F32)
    low = packed[:, nodes + gw_rows :].astype(F32)
    return grad_feat, (high + low).reshape(-1, width)


def solution(mesh):
    dp = mesh.shape["dp"]
    fine = Mesh(mesh.devices.reshape(dp, REP, ZH, ZL, YL), ("dp", "rep") + BLK)
    rows = ("dp",) + BLK
    return jax.shard_map(
        shards,
        mesh=fine,
        in_specs=(
            P(rows, None),
            P(rows, None),
            P(rows, None),
            P(),
            P(rows, "rep", None, None, None),
            P(rows, "rep", None),
            P(rows, "rep", None),
            P(rows, "rep"),
        ),
        out_specs=(P(rows, None), P(rows, None)),
        check_vma=False,
    )
```

```python
import functools

import jax
import jax.numpy as jnp
import numpy as np
from jax import lax
from jax.experimental import pallas as pl
from jax.experimental.pallas import tpu as pltpu
from jax.sharding import Mesh, PartitionSpec as P

ZH, ZL, YL, REP = 4, 4, 2, 4
BLK = ("zh", "zl", "yl")
BF16, F32 = jnp.bfloat16, jnp.float32


def contract_rows(left, right):
    return lax.dot_general(left, right, (((0,), (0,)), ((), ())), preferred_element_type=F32)


def hidden_order(width):
    units = np.arange(width).reshape(ZH * ZL * YL, REP, -1)
    return units.transpose(1, 2, 0).reshape(-1)


def dense_kernel(lane_ref, tiles_ref, *refs, places, masked):
    lists, refs = refs[:3], refs[3:]
    if masked:
        (pre_ref, up_ref, own_ref, *refs) = refs
        (*refs, pre_held, up_held, own_sems) = refs
        inputs = [
            pltpu.make_async_copy(source, held, own_sems.at[at])
            for at, (source, held) in enumerate(((pre_ref, pre_held), (up_ref, up_held)))
        ]
        for copy in inputs:
            copy.start()
    out_ref, rows_ref, cols_ref, count_ref, held_ref, acc_ref, sems, list_sems = refs
    _, slots, tile, _ = held_ref.shape
    fetches = [
        pltpu.make_async_copy(source, held, list_sems.at[at])
        for at, (source, held) in enumerate(zip(lists, (rows_ref, cols_ref, count_ref)))
    ]
    for fetch in fetches:
        fetch.start()
    last = tiles_ref.shape[1] // 2 - 1
    mirrored = lane_ref[0] >= REP // 2
    steps = [2 * jnp.where(mirrored, last - m, m) + odd for m, odd in places]
    copies = [
        pltpu.make_async_copy(tiles_ref.at[0, step], held_ref.at[at], sems.at[at])
        for at, step in enumerate(steps)
    ]
    for copy in copies:
        copy.start()
    if masked:
        for copy in inputs:
            copy.wait()
        own_ref[...] = jnp.where(pre_held[...] > 0, up_held[...], jnp.zeros_like(up_held))
    for fetch in fetches:
        fetch.wait()
    for at, step in enumerate(steps):
        acc_ref[...] = jnp.zeros_like(acc_ref)
        live = count_ref[0, step]
        copies[at].wait()
        for q in range(slots):

            @pl.when(q < live)
            def _():
                row, col = rows_ref[q, 0, step], cols_ref[q, 0, step]
                acc_ref[row, col] += held_ref[at, q].astype(F32)

        for row in range(2):
            for col in range(2):
                left = (2 * at + col) * tile
                out_ref[row * tile : (row + 1) * tile, left : left + tile] = acc_ref[
                    row, col
                ].astype(BF16)


def partial_kernel(even_ref, odd_ref, own_ref, next_ref, *out_refs, first):
    rows = even_ref.shape[0]
    for m, out_ref in enumerate(out_refs):
        span = slice(m * rows, (m + 1) * rows)
        far = slice((first + m) * rows, (first + m + 1) * rows)
        block = contract_rows(even_ref[:, far], own_ref[...])
        block += contract_rows(odd_ref[:, span], next_ref[...])
        out_ref[...] = block.astype(out_ref.dtype)


def near_kernel(keep_ref, first_ref, second_ref, third_ref, spread_ref, out_ref):
    total = keep_ref[...] + first_ref[...].astype(F32)
    total += second_ref[...].astype(F32) + third_ref[...].astype(F32)
    low = total.astype(BF16)
    quarter = out_ref.shape[2]
    for q in range(REP):
        span = slice(q * quarter, (q + 1) * quarter)
        out_ref[q] = jnp.dot(
            low, spread_ref[:, span], preferred_element_type=F32
        ).astype(BF16)


def weight_kernel(*refs, scale):
    *in_refs, feat_ref, p_ref, gw_ref, lines_ref = refs
    total = in_refs[0][...].astype(F32)
    for in_ref in in_refs[1:]:
        total += in_ref[...].astype(F32)
    p_ref[...] = total.astype(BF16)
    gw = contract_rows(p_ref[...], feat_ref[...]) * scale
    quarter = lines_ref.shape[1]
    spots = ZH * ZL * YL
    rows, pieces = gw.shape[0] // spots, gw.shape[1] // quarter
    for i in range(rows):
        for f in range(pieces):
            lines_ref[pl.ds(i * pieces + f, spots, rows * pieces), :] = gw[
                i * spots : (i + 1) * spots, f * quarter : (f + 1) * quarter
            ]
    gw_ref[...] = lines_ref[...].astype(BF16)


def pack_kernel(p_ref, gw_ref, out_ref):
    nodes, rows = p_ref.shape[0], gw_ref.shape[1]
    total = gw_ref[0].astype(F32)
    for d in range(1, gw_ref.shape[0]):
        total += gw_ref[d].astype(F32)
    high = total.astype(BF16)
    low = (total - high.astype(F32)).astype(BF16)
    for r in range(out_ref.shape[0]):
        out_ref[r, :nodes] = p_ref[...]
        out_ref[r, nodes : nodes + rows] = high
        out_ref[r, nodes + rows :] = low


def last_kernel(in_ref, weight_ref, feat_ref, gw_ref):
    nodes, width = feat_ref.shape
    quarter = in_ref.shape[2]
    lines = (in_ref.shape[1] - nodes) // 2
    pieces = width // quarter
    total = jnp.zeros(feat_ref.shape, F32)
    for q in range(REP):
        total += jnp.dot(
            in_ref[q, :nodes],
            weight_ref[q * quarter : (q + 1) * quarter, :],
            preferred_element_type=F32,
        )
        gw = in_ref[q, nodes : nodes + lines].astype(F32) + in_ref[q, nodes + lines :].astype(F32)
        for at in range(lines):
            row = q * (lines // pieces) + at // pieces
            left = at % pieces * quarter
            gw_ref[row : row + 1, left : left + quarter] = gw[at : at + 1, :]
    feat_ref[...] = total.astype(BF16)


def whole(kernel, outs, scalars, arrays, scratch=(), space=pltpu.VMEM, limit=48):
    return pl.pallas_call(
        kernel,
        in_specs=[pl.BlockSpec(memory_space=pltpu.SMEM)] * len(scalars)
        + [pl.BlockSpec(memory_space=space)] * len(arrays),
        out_specs=jax.tree.map(lambda _: pl.BlockSpec(memory_space=pltpu.VMEM), outs),
        out_shape=outs,
        scratch_shapes=scratch,
        compiler_params=pltpu.CompilerParams(vmem_limit_bytes=limit * 1024 * 1024),
    )(*scalars, *arrays)


def nothing(*refs):
    pass


def held_until(value, other):
    return pl.pallas_call(
        nothing,
        in_specs=[pl.BlockSpec(memory_space=pl.ANY), pl.BlockSpec(memory_space=pltpu.VMEM)],
        out_specs=pl.BlockSpec(memory_space=pl.ANY),
        out_shape=jax.ShapeDtypeStruct(value.shape, value.dtype),
        input_output_aliases={0: 0},
    )(value, other)


def exchange(value, axes):
    return lax.all_to_all(value, axes, 0, 0)


def to_previous(value):
    count = ZH * ZL * YL
    return lax.ppermute(value, BLK, [(b, (b - 1) % count) for b in range(count)])


def along_z(value, shifts):
    count = ZH * ZL
    pairs = [
        (r * count + z, r * count + (z + shift) % count)
        for r, shift in enumerate(shifts)
        for z in range(count)
    ]
    return lax.ppermute(value, ("rep", "zh", "zl"), pairs)


def shards(features, pre_act, upstream, weight, tile_values, tile_rows, tile_cols, tile_count):
    _, steps, slots, tile, _ = tile_values.shape
    nodes, width = features.shape
    hidden = upstream.shape[1]
    quarter = width // REP
    scale = float(nodes * ZH * ZL * YL) ** -0.5
    shape = jax.ShapeDtypeStruct
    lane = lax.axis_index("rep").reshape(1)

    lists = (tile_rows.transpose(2, 0, 1), tile_cols.transpose(2, 0, 1), tile_count)
    block = shape((nodes, hidden), BF16)

    def dense(places, masked=()):
        outs = (shape((2 * tile, len(places) * 2 * tile), BF16),)
        held = [pltpu.VMEM(value.shape, value.dtype) for value in masked]
        return whole(
            functools.partial(dense_kernel, places=places, masked=bool(masked)),
            ((block,) + outs) if masked else outs,
            (lane,),
            (tile_values, *lists, *masked),
            (
                *(pltpu.SMEM(listed.shape, listed.dtype) for listed in lists),
                pltpu.VMEM((len(places), slots, tile, tile), BF16),
                pltpu.VMEM((2, 2, tile, tile), F32),
                pltpu.SemaphoreType.DMA((len(places),)),
                pltpu.SemaphoreType.DMA((len(lists),)),
                *held,
                *((pltpu.SemaphoreType.DMA((len(held),)),) if held else ()),
            ),
            pltpu.HBM,
            60 if masked else 48,
        )

    def partial(odd, first, kinds):
        return whole(
            functools.partial(partial_kernel, first=first),
            tuple(shape((nodes, hidden), kind) for kind in kinds),
            (),
            (even, odd, own, following),
        )

    own, third_odd = dense(((3, 1),), (pre_act, upstream))
    even = dense(((0, 0), (1, 0), (2, 0), (3, 0)))[0]
    rest_odd = dense(((0, 1), (1, 1), (2, 1)))[0]
    following = to_previous(own)
    third_odd = to_previous(third_odd)
    third = partial(third_odd, 3, (BF16,))[0]
    rest_odd = to_previous(held_until(rest_odd, third))
    zeroth, keep, second = partial(rest_odd, 0, (BF16, F32, BF16))
    third = along_z(third, (-2, -2, 2, 2))
    second = along_z(second, (-1, -1, 1, 1))
    zeroth = along_z(zeroth, (1, 1, -1, -1))

    spread = np.zeros((hidden, hidden), np.float32)
    spread[hidden_order(hidden), np.arange(hidden)] = 1.0
    spread = jnp.asarray(spread, BF16)
    weight = contract_rows(spread, weight).astype(BF16)
    parts = whole(
        near_kernel,
        (shape((REP, nodes, quarter), BF16),),
        (),
        (keep, third, second, zeroth, spread),
    )[0]
    parts = exchange(parts, "rep")
    hops = (-1, -5, 6, 2)
    parts = [along_z(parts[r], (hops[r],) * REP) for r in (2, 1, 3, 0)]
    p_quarter, gw = whole(
        functools.partial(weight_kernel, scale=scale),
        (shape((nodes, quarter), BF16), shape((hidden, quarter), BF16)),
        (),
        (*parts, features),
        (pltpu.VMEM((hidden, quarter), F32),),
    )
    gw = exchange(gw.reshape(ZH * ZL * YL, -1, quarter), BLK)
    packed = whole(
        pack_kernel,
        (shape((REP, nodes + 2 * gw.shape[1], quarter), BF16),),
        (),
        (p_quarter, gw),
    )[0]
    packed = exchange(packed, "rep")
    return whole(
        last_kernel,
        (shape((nodes, width), BF16), shape((hidden // (ZH * ZL * YL), width), F32)),
        (),
        (packed, weight),
    )


def solution(mesh):
    dp = mesh.shape["dp"]
    fine = Mesh(mesh.devices.reshape(dp, REP, ZH, ZL, YL), ("dp", "rep") + BLK)
    rows = ("dp",) + BLK
    return jax.shard_map(
        shards,
        mesh=fine,
        in_specs=(
            P(rows, None),
            P(rows, None),
            P(rows, None),
            P(),
            P(rows, "rep", None, None, None),
            P(rows, "rep", None),
            P(rows, "rep", None),
            P(rows, "rep"),
        ),
        out_specs=(P(rows, None), P(rows, None)),
        check_vma=False,
    )
```

```python
import functools

import jax
import jax.numpy as jnp
import numpy as np
from jax import lax
from jax.experimental import pallas as pl
from jax.experimental.pallas import tpu as pltpu
from jax.sharding import Mesh, PartitionSpec as P

ZH, ZL, YL, REP = 4, 4, 2, 4
BLK = ("zh", "zl", "yl")
BF16, F32 = jnp.bfloat16, jnp.float32


def contract_rows(left, right):
    return lax.dot_general(left, right, (((0,), (0,)), ((), ())), preferred_element_type=F32)


def hidden_order(width):
    units = np.arange(width).reshape(ZH * ZL * YL, REP, -1)
    return units.transpose(1, 2, 0).reshape(-1)


def dense_kernel(tiles_ref, *refs, places, masked, marks):
    lists, refs = refs[:3], refs[3:]
    if masked:
        (pre_ref, up_ref, *refs) = refs
        (*refs, pre_held, up_held, own_sems) = refs
        inputs = [
            pltpu.make_async_copy(source, held, own_sems.at[at])
            for at, (source, held) in enumerate(((pre_ref, pre_held), (up_ref, up_held)))
        ]
        for copy in inputs:
            copy.start()
    out_ref, mark_ref, rows_ref, cols_ref, count_ref, held_ref, acc_ref, sems, list_sems = refs[marks:]
    mark_ref[...] = jnp.zeros_like(mark_ref)
    _, slots, tile, _ = held_ref.shape
    fetches = [
        pltpu.make_async_copy(source, held, list_sems.at[at])
        for at, (source, held) in enumerate(zip(lists, (rows_ref, cols_ref, count_ref)))
    ]
    for fetch in fetches:
        fetch.start()
    steps = [2 * m + odd for m, odd in places]
    copies = [
        pltpu.make_async_copy(tiles_ref.at[0, step], held_ref.at[at], sems.at[at])
        for at, step in enumerate(steps)
    ]
    for copy in copies:
        copy.start()
    if masked:
        for copy in inputs:
            copy.wait()
        own = jnp.where(pre_held[...] > 0, up_held[...], jnp.zeros_like(up_held))
        out_ref[:, : own.shape[1]] = own
    for fetch in fetches:
        fetch.wait()
    for at, step in enumerate(steps):
        acc_ref[...] = jnp.zeros_like(acc_ref)
        live = count_ref[0, step]
        copies[at].wait()
        for q in range(slots):

            @pl.when(q < live)
            def _():
                row, col = rows_ref[q, 0, step], cols_ref[q, 0, step]
                acc_ref[row, col] += held_ref[at, q].astype(F32)

        for row in range(2):
            for col in range(2):
                left = out_ref.shape[1] + (2 * (at - len(places)) + col) * tile
                out_ref[row * tile : (row + 1) * tile, left : left + tile] = acc_ref[
                    row, col
                ].astype(BF16)


def partial_kernel(even_ref, own_ref, next_ref, *refs, first, kinds):
    rows = even_ref.shape[0]
    *refs, mark_ref = refs
    mark_ref[...] = jnp.zeros_like(mark_ref)
    out_refs = refs[len(refs) - kinds :]
    hidden = out_refs[0].shape[1]
    odd = refs[0][...] if first else next_ref[:, hidden:]
    for m, out_ref in enumerate(out_refs):
        span = slice(m * rows, (m + 1) * rows)
        far = slice((first + m) * rows, (first + m + 1) * rows)
        block = contract_rows(even_ref[:, far], own_ref[:, :hidden])
        block += contract_rows(odd[:, span], next_ref[:, :hidden])
        out_ref[...] = block.astype(out_ref.dtype)


def near_kernel(some_ref, first_ref, second_ref, spread_ref, out_ref):
    total = some_ref[...] + first_ref[...].astype(F32) + second_ref[...].astype(F32)
    low = total.astype(BF16)
    quarter = out_ref.shape[2]
    for q in range(REP):
        span = slice(q * quarter, (q + 1) * quarter)
        out_ref[q] = jnp.dot(
            low, spread_ref[:, span], preferred_element_type=F32
        ).astype(BF16)


def sum_kernel(left_ref, right_ref, out_ref):
    out_ref[...] = left_ref[...].astype(F32) + right_ref[...].astype(F32)


def weight_kernel(*refs, scale):
    *in_refs, feat_ref, p_ref, gw_ref, lines_ref = refs
    total = in_refs[0][...].astype(F32)
    for in_ref in in_refs[1:]:
        total += in_ref[...].astype(F32)
    p_ref[...] = total.astype(BF16)
    gw = contract_rows(p_ref[...], feat_ref[...]) * scale
    quarter = lines_ref.shape[1]
    spots = ZH * ZL * YL
    rows, pieces = gw.shape[0] // spots, gw.shape[1] // quarter
    for i in range(rows):
        for f in range(pieces):
            lines_ref[pl.ds(i * pieces + f, spots, rows * pieces), :] = gw[
                i * spots : (i + 1) * spots, f * quarter : (f + 1) * quarter
            ]
    gw_ref[...] = lines_ref[...].astype(BF16)


def feature_kernel(lane_ref, *refs):
    *in_refs, weight_ref, feat_ref = refs
    quarter = in_refs[0].shape[1]
    total = jnp.zeros(feat_ref.shape, F32)
    for back, in_ref in enumerate(in_refs):
        source = lax.rem(lane_ref[0] + REP - back, REP)
        span = pl.ds(pl.multiple_of(source * quarter, quarter), quarter)
        total += jnp.dot(in_ref[...], weight_ref[span, :], preferred_element_type=F32)
    feat_ref[...] = total.astype(BF16)


def copies_kernel(in_ref, out_ref):
    total = in_ref[0].astype(F32)
    for d in range(1, in_ref.shape[0]):
        total += in_ref[d].astype(F32)
    for r in range(out_ref.shape[0]):
        out_ref[r] = total


def lines_kernel(in_ref, gw_ref):
    lanes, lines, quarter = in_ref.shape
    pieces = gw_ref.shape[1] // quarter
    for q in range(lanes):
        for at in range(lines):
            row = q * (lines // pieces) + at // pieces
            left = at % pieces * quarter
            gw_ref[row : row + 1, left : left + quarter] = in_ref[q, at : at + 1, :]


def whole(kernel, outs, scalars, arrays, scratch=(), space=pltpu.VMEM, limit=48):
    return pl.pallas_call(
        kernel,
        in_specs=[pl.BlockSpec(memory_space=pltpu.SMEM)] * len(scalars)
        + [pl.BlockSpec(memory_space=space)] * len(arrays),
        out_specs=jax.tree.map(lambda _: pl.BlockSpec(memory_space=pltpu.VMEM), outs),
        out_shape=outs,
        scratch_shapes=scratch,
        compiler_params=pltpu.CompilerParams(vmem_limit_bytes=limit * 1024 * 1024),
    )(*scalars, *arrays)


def exchange(value, axes):
    return lax.all_to_all(value, axes, 0, 0)


def to_previous(value):
    count = ZH * ZL * YL
    return lax.ppermute(value, BLK, [(b, (b - 1) % count) for b in range(count)])


def along_z(value, shift):
    count = ZH * ZL
    return lax.ppermute(value, ("zh", "zl"), [(z, (z + shift) % count) for z in range(count)])


def shards(features, pre_act, upstream, weight, tile_values, tile_rows, tile_cols, tile_count):
    _, steps, slots, tile, _ = tile_values.shape
    nodes, width = features.shape
    hidden = upstream.shape[1]
    quarter = width // REP
    scale = float(nodes * ZH * ZL * YL) ** -0.5
    shape = jax.ShapeDtypeStruct

    lists = (tile_rows.transpose(2, 0, 1), tile_cols.transpose(2, 0, 1), tile_count)
    mark = shape((8, tile), F32)

    def dense(places, masked=(), marks=()):
        wide = len(places) * 2 * tile + (hidden if masked else 0)
        outs = (shape((nodes, wide), BF16), mark)
        held = [pltpu.VMEM(value.shape, value.dtype) for value in masked]
        return whole(
            functools.partial(
                dense_kernel, places=places, masked=bool(masked), marks=len(marks)
            ),
            outs,
            (),
            (tile_values, *lists, *masked, *marks),
            (
                *(pltpu.SMEM(listed.shape, listed.dtype) for listed in lists),
                pltpu.VMEM((len(places), slots, tile, tile), BF16),
                pltpu.VMEM((2, 2, tile, tile), F32),
                pltpu.SemaphoreType.DMA((len(places),)),
                pltpu.SemaphoreType.DMA((len(lists),)),
                *held,
                *((pltpu.SemaphoreType.DMA((len(held),)),) if held else ()),
            ),
            pltpu.HBM,
            60 if masked else 48,
        )

    def partial(odd, first, kinds):
        return whole(
            functools.partial(partial_kernel, first=first, kinds=len(kinds)),
            tuple(shape((nodes, hidden), kind) for kind in kinds) + (mark,),
            (),
            (even, first_part, following, *odd),
        )

    first_part, mark_first = dense(((0, 1),), (pre_act, upstream))
    even, mark_even = dense(((0, 0), (1, 0), (2, 0), (3, 0)), marks=(mark_first,))
    rest_odd, _ = dense(((1, 1), (2, 1), (3, 1)), marks=(mark_even,))
    following = to_previous(first_part)
    rest_odd = to_previous(rest_odd)
    two, mark_two = partial((), 0, (BF16,))
    one, keep, back, _ = partial((rest_odd, mark_two), 1, (BF16, F32, BF16))
    some = whole(sum_kernel, (shape((nodes, hidden), F32),), (), (keep, along_z(two, 2)))[0]
    one = along_z(one, 1)
    back = along_z(back, -1)

    spread = np.zeros((hidden, hidden), np.float32)
    spread[hidden_order(hidden), np.arange(hidden)] = 1.0
    spread = jnp.asarray(spread, BF16)
    weight = contract_rows(spread, weight).astype(BF16)
    parts = whole(
        near_kernel,
        (shape((REP, nodes, quarter), BF16),),
        (),
        (some, one, back, spread),
    )[0]
    parts = exchange(parts, "rep")
    hops = (-2, -6, 6, 2)
    parts = [along_z(parts[r], hops[r]) for r in range(REP)]
    far = whole(sum_kernel, (shape((nodes, quarter), F32),), (), (parts[1], parts[2]))[0]
    p_quarter, gw = whole(
        functools.partial(weight_kernel, scale=scale),
        (shape((nodes, quarter), BF16), shape((hidden, quarter), BF16)),
        (),
        (far, parts[0], parts[3], features),
        (pltpu.VMEM((hidden, quarter), F32),),
    )
    gw = exchange(gw.reshape(ZH * ZL * YL, -1, quarter), BLK)
    gw = whole(copies_kernel, (shape((REP,) + gw.shape[1:], F32),), (), (gw,))[0]
    gw = exchange(gw, "rep")
    lane = lax.axis_index("rep").reshape(1)
    p_all = [p_quarter] + [
        lax.ppermute(p_quarter, "rep", [(r, (r + back) % REP) for r in range(REP)])
        for back in range(1, REP)
    ]
    grad_feat = whole(
        feature_kernel, (shape((nodes, width), BF16),), (lane,), (*p_all, weight)
    )[0]
    rows = hidden // (ZH * ZL * YL)
    grad_weight = whole(lines_kernel, (shape((rows, width), F32),), (), (gw,))[0]
    return grad_feat, grad_weight


def solution(mesh):
    dp = mesh.shape["dp"]
    fine = Mesh(mesh.devices.reshape(dp, REP, ZH, ZL, YL), ("dp", "rep") + BLK)
    rows = ("dp",) + BLK
    return jax.shard_map(
        shards,
        mesh=fine,
        in_specs=(
            P(rows, None),
            P(rows, None),
            P(rows, None),
            P(),
            P(rows, "rep", None, None, None),
            P(rows, "rep", None),
            P(rows, "rep", None),
            P(rows, "rep"),
        ),
        out_specs=(P(rows, None), P(rows, None)),
        check_vma=False,
    )
```

```python
import functools

import jax
import jax.numpy as jnp
import numpy as np
from jax import lax
from jax.experimental import pallas as pl
from jax.experimental.pallas import tpu as pltpu
from jax.sharding import Mesh, PartitionSpec as P

ZH, ZL, YL, REP = 4, 4, 2, 4
BLK = ("zh", "zl", "yl")
BF16, F32 = jnp.bfloat16, jnp.float32


def contract_rows(left, right):
    return lax.dot_general(left, right, (((0,), (0,)), ((), ())), preferred_element_type=F32)


def hidden_order(width):
    units = np.arange(width).reshape(ZH * ZL * YL, REP, -1)
    return units.transpose(1, 2, 0).reshape(-1)


def dense_kernel(tiles_ref, *refs, places, masked, marks):
    lists, refs = refs[:3], refs[3:]
    if masked:
        (pre_ref, up_ref, *refs) = refs
        (*refs, pre_held, up_held, own_sems) = refs
        inputs = [
            pltpu.make_async_copy(source, held, own_sems.at[at])
            for at, (source, held) in enumerate(((pre_ref, pre_held), (up_ref, up_held)))
        ]
        for copy in inputs:
            copy.start()
    out_ref, mark_ref, rows_ref, cols_ref, count_ref, held_ref, acc_ref, sems, list_sems = refs[marks:]
    mark_ref[...] = jnp.zeros_like(mark_ref)
    _, slots, tile, _ = held_ref.shape
    fetches = [
        pltpu.make_async_copy(source, held, list_sems.at[at])
        for at, (source, held) in enumerate(zip(lists, (rows_ref, cols_ref, count_ref)))
    ]
    for fetch in fetches:
        fetch.start()
    steps = [2 * m + odd for m, odd in places]
    copies = [
        pltpu.make_async_copy(tiles_ref.at[0, step], held_ref.at[at], sems.at[at])
        for at, step in enumerate(steps)
    ]
    for copy in copies:
        copy.start()
    if masked:
        for copy in inputs:
            copy.wait()
        own = jnp.where(pre_held[...] > 0, up_held[...], jnp.zeros_like(up_held))
        out_ref[:, : own.shape[1]] = own
    for fetch in fetches:
        fetch.wait()
    for at, step in enumerate(steps):
        acc_ref[...] = jnp.zeros_like(acc_ref)
        live = count_ref[0, step]
        copies[at].wait()
        for q in range(slots):

            @pl.when(q < live)
            def _():
                row, col = rows_ref[q, 0, step], cols_ref[q, 0, step]
                acc_ref[row, col] += held_ref[at, q].astype(F32)

        for row in range(2):
            for col in range(2):
                left = out_ref.shape[1] + (2 * (at - len(places)) + col) * tile
                out_ref[row * tile : (row + 1) * tile, left : left + tile] = acc_ref[
                    row, col
                ].astype(BF16)


def partial_kernel(even_ref, own_ref, next_ref, *refs, first, kinds):
    rows = even_ref.shape[0]
    *refs, mark_ref = refs
    mark_ref[...] = jnp.zeros_like(mark_ref)
    out_refs = refs[len(refs) - kinds :]
    hidden = out_refs[0].shape[1]
    odd = refs[0][...] if first else next_ref[:, hidden:]
    for m, out_ref in enumerate(out_refs):
        span = slice(m * rows, (m + 1) * rows)
        far = slice((first + m) * rows, (first + m + 1) * rows)
        block = contract_rows(even_ref[:, far], own_ref[:, :hidden])
        block += contract_rows(odd[:, span], next_ref[:, :hidden])
        out_ref[...] = block.astype(out_ref.dtype)


def near_kernel(some_ref, first_ref, second_ref, spread_ref, out_ref):
    total = some_ref[...] + first_ref[...].astype(F32) + second_ref[...].astype(F32)
    low = total.astype(BF16)
    quarter = out_ref.shape[2]
    for q in range(REP):
        span = slice(q * quarter, (q + 1) * quarter)
        out_ref[q] = jnp.dot(
            low, spread_ref[:, span], preferred_element_type=F32
        ).astype(BF16)


def sum_kernel(left_ref, right_ref, out_ref):
    total = left_ref[...].astype(F32) + right_ref[...].astype(F32)
    out_ref[...] = total.astype(out_ref.dtype)


def weight_kernel(*refs, scale):
    *in_refs, feat_ref, p_ref, gw_ref, lines_ref = refs
    total = in_refs[0][...].astype(F32)
    for in_ref in in_refs[1:]:
        total += in_ref[...].astype(F32)
    p_ref[...] = total.astype(BF16)
    gw = contract_rows(p_ref[...], feat_ref[...]) * scale
    quarter = lines_ref.shape[1]
    spots = ZH * ZL * YL
    rows, pieces = gw.shape[0] // spots, gw.shape[1] // quarter
    for i in range(rows):
        for f in range(pieces):
            lines_ref[pl.ds(i * pieces + f, spots, rows * pieces), :] = gw[
                i * spots : (i + 1) * spots, f * quarter : (f + 1) * quarter
            ]
    gw_ref[...] = lines_ref[...].astype(BF16)


def feature_kernel(lane_ref, *refs):
    *in_refs, weight_ref, feat_ref = refs
    quarter = in_refs[0].shape[1]
    total = jnp.zeros(feat_ref.shape, F32)
    for back, in_ref in enumerate(in_refs):
        source = lax.rem(lane_ref[0] + REP - back, REP)
        span = pl.ds(pl.multiple_of(source * quarter, quarter), quarter)
        total += jnp.dot(in_ref[...], weight_ref[span, :], preferred_element_type=F32)
    feat_ref[...] = total.astype(BF16)


def copies_kernel(in_ref, out_ref):
    total = in_ref[0].astype(F32)
    for d in range(1, in_ref.shape[0]):
        total += in_ref[d].astype(F32)
    for r in range(out_ref.shape[0]):
        out_ref[r] = total


def lines_kernel(in_ref, gw_ref):
    lanes, lines, quarter = in_ref.shape
    pieces = gw_ref.shape[1] // quarter
    for q in range(lanes):
        for at in range(lines):
            row = q * (lines // pieces) + at // pieces
            left = at % pieces * quarter
            gw_ref[row : row + 1, left : left + quarter] = in_ref[q, at : at + 1, :]


def whole(kernel, outs, scalars, arrays, scratch=(), space=pltpu.VMEM, limit=48):
    return pl.pallas_call(
        kernel,
        in_specs=[pl.BlockSpec(memory_space=pltpu.SMEM)] * len(scalars)
        + [pl.BlockSpec(memory_space=space)] * len(arrays),
        out_specs=jax.tree.map(lambda _: pl.BlockSpec(memory_space=pltpu.VMEM), outs),
        out_shape=outs,
        scratch_shapes=scratch,
        compiler_params=pltpu.CompilerParams(vmem_limit_bytes=limit * 1024 * 1024),
    )(*scalars, *arrays)


def exchange(value, axes):
    return lax.all_to_all(value, axes, 0, 0)


def to_previous(value):
    count = ZH * ZL * YL
    return lax.ppermute(value, BLK, [(b, (b - 1) % count) for b in range(count)])


def along_z(value, shift):
    count = ZH * ZL
    return lax.ppermute(value, ("zh", "zl"), [(z, (z + shift) % count) for z in range(count)])


def shards(features, pre_act, upstream, weight, tile_values, tile_rows, tile_cols, tile_count):
    _, steps, slots, tile, _ = tile_values.shape
    nodes, width = features.shape
    hidden = upstream.shape[1]
    quarter = width // REP
    scale = float(nodes * ZH * ZL * YL) ** -0.5
    shape = jax.ShapeDtypeStruct

    lists = (tile_rows.transpose(2, 0, 1), tile_cols.transpose(2, 0, 1), tile_count)
    mark = shape((8, tile), F32)

    def dense(places, masked=(), marks=()):
        wide = len(places) * 2 * tile + (hidden if masked else 0)
        outs = (shape((nodes, wide), BF16), mark)
        held = [pltpu.VMEM(value.shape, value.dtype) for value in masked]
        return whole(
            functools.partial(
                dense_kernel, places=places, masked=bool(masked), marks=len(marks)
            ),
            outs,
            (),
            (tile_values, *lists, *masked, *marks),
            (
                *(pltpu.SMEM(listed.shape, listed.dtype) for listed in lists),
                pltpu.VMEM((len(places), slots, tile, tile), BF16),
                pltpu.VMEM((2, 2, tile, tile), F32),
                pltpu.SemaphoreType.DMA((len(places),)),
                pltpu.SemaphoreType.DMA((len(lists),)),
                *held,
                *((pltpu.SemaphoreType.DMA((len(held),)),) if held else ()),
            ),
            pltpu.HBM,
            60 if masked else 48,
        )

    def partial(odd, first, kinds):
        return whole(
            functools.partial(partial_kernel, first=first, kinds=len(kinds)),
            tuple(shape((nodes, hidden), kind) for kind in kinds) + (mark,),
            (),
            (even, first_part, following, *odd),
        )

    first_part, mark_first = dense(((0, 1),), (pre_act, upstream))
    even, mark_even = dense(((0, 0), (1, 0), (2, 0), (3, 0)), marks=(mark_first,))
    rest_odd, _ = dense(((1, 1), (2, 1), (3, 1)), marks=(mark_even,))
    following = to_previous(first_part)
    rest_odd = to_previous(rest_odd)
    two, mark_two = partial((), 0, (BF16,))
    one, keep, back, _ = partial((rest_odd, mark_two), 1, (F32, F32, BF16))
    two = along_z(two, 1)
    one = along_z(whole(sum_kernel, (shape((nodes, hidden), BF16),), (), (one, two))[0], 1)
    back = along_z(back, -1)

    spread = np.zeros((hidden, hidden), np.float32)
    spread[hidden_order(hidden), np.arange(hidden)] = 1.0
    spread = jnp.asarray(spread, BF16)
    weight = contract_rows(spread, weight).astype(BF16)
    parts = whole(
        near_kernel,
        (shape((REP, nodes, quarter), BF16),),
        (),
        (keep, one, back, spread),
    )[0]
    parts = exchange(parts, "rep")
    hops = (-2, -6, 6, 2)
    parts = [along_z(parts[r], hops[r]) for r in range(REP)]
    far = whole(sum_kernel, (shape((nodes, quarter), F32),), (), (parts[1], parts[2]))[0]
    p_quarter, gw = whole(
        functools.partial(weight_kernel, scale=scale),
        (shape((nodes, quarter), BF16), shape((hidden, quarter), BF16)),
        (),
        (far, parts[0], parts[3], features),
        (pltpu.VMEM((hidden, quarter), F32),),
    )
    gw = exchange(gw.reshape(ZH * ZL * YL, -1, quarter), BLK)
    gw = whole(copies_kernel, (shape((REP,) + gw.shape[1:], F32),), (), (gw,))[0]
    gw = exchange(gw, "rep")
    lane = lax.axis_index("rep").reshape(1)
    p_all = [p_quarter] + [
        lax.ppermute(p_quarter, "rep", [(r, (r + back) % REP) for r in range(REP)])
        for back in range(1, REP)
    ]
    grad_feat = whole(
        feature_kernel, (shape((nodes, width), BF16),), (lane,), (*p_all, weight)
    )[0]
    rows = hidden // (ZH * ZL * YL)
    grad_weight = whole(lines_kernel, (shape((rows, width), F32),), (), (gw,))[0]
    return grad_feat, grad_weight


def solution(mesh):
    dp = mesh.shape["dp"]
    fine = Mesh(mesh.devices.reshape(dp, REP, ZH, ZL, YL), ("dp", "rep") + BLK)
    rows = ("dp",) + BLK
    return jax.shard_map(
        shards,
        mesh=fine,
        in_specs=(
            P(rows, None),
            P(rows, None),
            P(rows, None),
            P(),
            P(rows, "rep", None, None, None),
            P(rows, "rep", None),
            P(rows, "rep", None),
            P(rows, "rep"),
        ),
        out_specs=(P(rows, None), P(rows, None)),
        check_vma=False,
    )
```

```python
import functools

import jax
import jax.numpy as jnp
import numpy as np
from jax import lax
from jax.experimental import pallas as pl
from jax.experimental.pallas import tpu as pltpu
from jax.sharding import Mesh, PartitionSpec as P

ZH, ZL, YL, REP = 4, 4, 2, 4
BLK = ("zh", "zl", "yl")
BF16, F32 = jnp.bfloat16, jnp.float32


def contract_rows(left, right):
    return lax.dot_general(left, right, (((0,), (0,)), ((), ())), preferred_element_type=F32)


def hidden_order(width):
    units = np.arange(width).reshape(ZH * ZL * YL, REP, -1)
    return units.transpose(1, 2, 0).reshape(-1)


def masked(pre_act, upstream):
    return jnp.where(pre_act > 0, upstream, jnp.zeros_like(upstream))


def step_of(odd, role, yl, last):
    return 2 * jnp.where(yl == 0, last - role, role) + 1 if odd else 2 * role


def term(tile_at, rows_ref, cols_ref, count_ref, step, own, out_ref, acc_ref):
    acc_ref[...] = jnp.zeros_like(acc_ref)
    live = count_ref[0, step]
    for q in range(rows_ref.shape[0]):

        @pl.when(q < live)
        def _():
            acc_ref[rows_ref[q, 0, step], cols_ref[q, 0, step]] += tile_at(q).astype(F32)

    dense = jnp.concatenate(
        [jnp.concatenate([acc_ref[row, col] for col in range(2)], axis=1) for row in range(2)],
        axis=0,
    ).astype(BF16)
    out_ref[...] = contract_rows(dense, own).astype(out_ref.dtype)


def first_kernel(yl_ref, *refs, odd, role):
    tiles_ref, *sources, out_ref, held_ref = refs[:8]
    *held, acc_ref, sems = refs[8:]
    step = step_of(odd, role, yl_ref[0], tiles_ref.shape[1] // 2 - 1)
    copies = [
        pltpu.make_async_copy(source, kept, sems.at[at])
        for at, (source, kept) in enumerate(
            [*zip(sources, held), (tiles_ref.at[0, step], held_ref)]
        )
    ]
    for copy in copies:
        copy.start()
    for copy in copies:
        copy.wait()
    rows_ref, cols_ref, count_ref, pre_ref, up_ref = held
    own = masked(pre_ref[...], up_ref[...])
    term(lambda q: held_ref[q], rows_ref, cols_ref, count_ref, step, own, out_ref, acc_ref)


def terms_kernel(yl_ref, rows_ref, cols_ref, count_ref, tiles_ref, pre_ref, up_ref, *refs, roles):
    *out_refs, mark_ref, acc_ref, own_ref = refs[len(refs) - len(roles) - 3 :]
    mark_ref[...] = jnp.zeros_like(mark_ref)
    own_ref[...] = masked(pre_ref[...], up_ref[...])
    last = tiles_ref.shape[1] // 2 - 1
    for (odd, role), out_ref in zip(roles, out_refs):
        step = step_of(odd, role, yl_ref[0], last)
        term(
            lambda q: tiles_ref[0, step, q],
            rows_ref,
            cols_ref,
            count_ref,
            step,
            own_ref[...],
            out_ref,
            acc_ref,
        )


def gather_kernel(keep_ref, first_ref, second_ref, out_ref):
    total = keep_ref[...] + first_ref[...].astype(F32) + second_ref[...].astype(F32)
    out_ref[...] = total.astype(BF16)


def near_kernel(yl_ref, other_ref, keep_ref, first_ref, second_ref, spread_ref, out_ref):
    quarter = out_ref.shape[2]
    total = keep_ref[...] + first_ref[...].astype(F32) + second_ref[...].astype(F32)
    for low, lane in ((total.astype(BF16), yl_ref[0]), (other_ref[...], 1 - yl_ref[0])):
        for q in range(REP):
            span = slice(q * quarter, (q + 1) * quarter)
            out_ref[YL * q + lane] = jnp.dot(
                low, spread_ref[:, span], preferred_element_type=F32
            ).astype(BF16)


def sides_kernel(in_ref, *out_refs):
    for r, out_ref in enumerate(out_refs):
        total = in_ref[YL * r].astype(F32)
        for side in range(1, YL):
            total += in_ref[YL * r + side].astype(F32)
        out_ref[...] = total.astype(BF16)


def sum_kernel(left_ref, right_ref, out_ref, *mark_refs):
    for mark_ref in mark_refs:
        mark_ref[...] = jnp.zeros_like(mark_ref)
    total = left_ref[...].astype(F32) + right_ref[...].astype(F32)
    out_ref[...] = total.astype(out_ref.dtype)


def weight_kernel(*refs, scale):
    *in_refs, feat_ref, p_ref, gw_ref, lines_ref = refs
    total = in_refs[0][...].astype(F32)
    for in_ref in in_refs[1:]:
        total += in_ref[...].astype(F32)
    p_ref[...] = total.astype(BF16)
    gw = contract_rows(p_ref[...], feat_ref[...]) * scale
    quarter = lines_ref.shape[1]
    spots = ZH * ZL * YL
    rows, pieces = gw.shape[0] // spots, gw.shape[1] // quarter
    for i in range(rows):
        for f in range(pieces):
            lines_ref[pl.ds(f * rows + i, spots, rows * pieces), :] = gw[
                i * spots : (i + 1) * spots, f * quarter : (f + 1) * quarter
            ]
    gw_ref[...] = lines_ref[...].astype(BF16)


def pair_kernel(own_ref, other_ref, out_ref):
    out_ref[0] = own_ref[...]
    out_ref[1] = other_ref[...]


def feature_kernel(lane_ref, own_ref, other_ref, weight_ref, feat_ref):
    quarter = own_ref.shape[2]
    total = jnp.zeros(feat_ref.shape, F32)
    for at in range(REP):
        source = lane_ref[0] ^ at
        span = pl.ds(pl.multiple_of(source * quarter, quarter), quarter)
        part = (own_ref if at < 2 else other_ref)[at % 2]
        total += jnp.dot(part, weight_ref[span, :], preferred_element_type=F32)
    feat_ref[...] = total.astype(BF16)


def copies_kernel(in_ref, out_ref):
    total = in_ref[0].astype(F32)
    for d in range(1, in_ref.shape[0]):
        total += in_ref[d].astype(F32)
    for r in range(out_ref.shape[0]):
        out_ref[r] = total


def lines_kernel(in_ref, gw_ref):
    lanes, lines, quarter = in_ref.shape
    pieces = gw_ref.shape[1] // quarter
    rows = lines // pieces
    for q in range(lanes):
        for f in range(pieces):
            gw_ref[q * rows : (q + 1) * rows, f * quarter : (f + 1) * quarter] = in_ref[
                q, f * rows : (f + 1) * rows, :
            ]


def whole(kernel, outs, scalars, arrays, scratch=(), space=pltpu.VMEM, limit=48):
    return pl.pallas_call(
        kernel,
        in_specs=[pl.BlockSpec(memory_space=pltpu.SMEM)] * len(scalars)
        + [pl.BlockSpec(memory_space=space)] * len(arrays),
        out_specs=jax.tree.map(lambda _: pl.BlockSpec(memory_space=pltpu.VMEM), outs),
        out_shape=outs,
        scratch_shapes=scratch,
        compiler_params=pltpu.CompilerParams(vmem_limit_bytes=limit * 1024 * 1024),
    )(*scalars, *arrays)


def exchange(value, axes):
    return lax.all_to_all(value, axes, 0, 0)


def along_z(value, shift):
    count = ZH * ZL
    return lax.ppermute(value, ("zh", "zl"), [(z, (z + shift) % count) for z in range(count)])


def turned_along_z(value, shift):
    count = ZH * ZL
    pairs = [
        (z * YL + y, (z + (shift if y else -shift)) % count * YL + y)
        for z in range(count)
        for y in range(YL)
    ]
    return lax.ppermute(value, BLK, pairs)


def shards(features, pre_act, upstream, weight, tile_values, tile_rows, tile_cols, tile_count):
    _, steps, slots, tile, _ = tile_values.shape
    nodes, width = features.shape
    hidden = upstream.shape[1]
    quarter = width // REP
    scale = float(nodes * ZH * ZL * YL) ** -0.5
    shape = jax.ShapeDtypeStruct

    lists = (tile_rows.transpose(2, 0, 1), tile_cols.transpose(2, 0, 1), tile_count)
    mark = shape((8, tile), F32)

    yl = lax.axis_index("yl").reshape(1)

    gates = (pre_act, upstream)
    block = shape((nodes, hidden), BF16)
    acc = pltpu.VMEM((2, 2, tile, tile), F32)

    def terms(roles, kinds, marks=()):
        return whole(
            functools.partial(terms_kernel, roles=roles),
            tuple(shape((nodes, hidden), kind) for kind in kinds) + (mark,),
            (yl, *lists),
            (tile_values, *gates, *marks),
            (acc, pltpu.VMEM(block.shape, block.dtype)),
        )

    far_other = whole(
        functools.partial(first_kernel, odd=1, role=0),
        (block,),
        (yl,),
        (tile_values, *lists, *gates),
        (
            pltpu.VMEM((slots, tile, tile), BF16),
            *(pltpu.SMEM(listed.shape, listed.dtype) for listed in lists),
            *(pltpu.VMEM(gate.shape, gate.dtype) for gate in gates),
            acc,
            pltpu.SemaphoreType.DMA((6,)),
        ),
        pltpu.HBM,
        60,
    )[0]
    far_same, back_other, mid_other, _ = terms(((0, 0), (1, 3), (1, 1)), (BF16, BF16, F32))
    mid_other, mark_other = whole(
        sum_kernel, (block, mark), (), (mid_other, turned_along_z(far_other, 1))
    )
    mid_same, back_same, keep_other, keep_same, _ = terms(
        ((0, 1), (0, 3), (1, 2), (0, 2)), (F32, BF16, F32, F32), (mark_other,)
    )
    mid_same = whole(sum_kernel, (block,), (), (mid_same, along_z(far_same, 1)))[0]
    mid_other = turned_along_z(mid_other, 1)
    back_other = turned_along_z(back_other, -1)
    mid_same = along_z(mid_same, 1)
    back_same = along_z(back_same, -1)
    other = whole(gather_kernel, (block,), (), (keep_other, mid_other, back_other))[0]

    spread = np.zeros((hidden, hidden), np.float32)
    spread[hidden_order(hidden), np.arange(hidden)] = 1.0
    spread = jnp.asarray(spread, BF16)
    weight = contract_rows(spread, weight).astype(BF16)
    parts = whole(
        near_kernel,
        (shape((REP * YL, nodes, quarter), BF16),),
        (yl,),
        (other, keep_same, mid_same, back_same, spread),
    )[0]
    parts = exchange(parts, ("rep", "yl"))
    parts = whole(sides_kernel, (shape((nodes, quarter), BF16),) * REP, (), (parts,))
    hops = (-2, -6, 6, 2)
    parts = [along_z(parts[r], hops[r]) for r in range(REP)]
    far = whole(sum_kernel, (shape((nodes, quarter), F32),), (), (parts[1], parts[2]))[0]
    p_quarter, gw = whole(
        functools.partial(weight_kernel, scale=scale),
        (shape((nodes, quarter), BF16), shape((hidden, quarter), BF16)),
        (),
        (far, parts[0], parts[3], features),
        (pltpu.VMEM((hidden, quarter), F32),),
    )
    gw = exchange(gw.reshape(ZH * ZL * YL, -1, quarter), BLK)
    gw = whole(copies_kernel, (shape((REP,) + gw.shape[1:], F32),), (), (gw,))[0]
    gw = exchange(gw, "rep")
    lane = lax.axis_index("rep").reshape(1)
    other = lax.ppermute(p_quarter, "rep", [(r, r ^ 1) for r in range(REP)])
    pair = whole(pair_kernel, (shape((2, nodes, quarter), BF16),), (), (p_quarter, other))[0]
    others = lax.ppermute(pair, "rep", [(r, r ^ 2) for r in range(REP)])
    grad_feat = whole(
        feature_kernel, (shape((nodes, width), BF16),), (lane,), (pair, others, weight)
    )[0]
    rows = hidden // (ZH * ZL * YL)
    grad_weight = whole(lines_kernel, (shape((rows, width), F32),), (), (gw,))[0]
    return grad_feat, grad_weight


def solution(mesh):
    dp = mesh.shape["dp"]
    fine = Mesh(mesh.devices.reshape(dp, REP, ZH, ZL, YL), ("dp", "rep") + BLK)
    rows = ("dp",) + BLK
    return jax.shard_map(
        shards,
        mesh=fine,
        in_specs=(
            P(rows, None),
            P(rows, None),
            P(rows, None),
            P(),
            P(rows, "rep", None, None, None),
            P(rows, "rep", None),
            P(rows, "rep", None),
            P(rows, "rep"),
        ),
        out_specs=(P(rows, None), P(rows, None)),
        check_vma=False,
    )
```

```python
import functools

import jax
import jax.numpy as jnp
import numpy as np
from jax import lax
from jax.experimental import pallas as pl
from jax.experimental.pallas import tpu as pltpu
from jax.sharding import Mesh, PartitionSpec as P

ZH, ZL, YL, REP = 4, 4, 2, 4
BLK = ("zh", "zl", "yl")
BF16, F32 = jnp.bfloat16, jnp.float32


def contract_rows(left, right):
    return lax.dot_general(left, right, (((0,), (0,)), ((), ())), preferred_element_type=F32)


def hidden_order(width):
    units = np.arange(width).reshape(ZH * ZL * YL, REP, -1)
    return units.transpose(1, 2, 0).reshape(-1)


def masked(pre_act, upstream):
    return jnp.where(pre_act > 0, upstream, jnp.zeros_like(upstream))


def step_of(odd, role, yl, last):
    return 2 * jnp.where(yl == 0, last - role, role) + 1 if odd else 2 * role


def term(tile_at, rows_ref, cols_ref, count_ref, step, own, out_ref, acc_ref):
    acc_ref[...] = jnp.zeros_like(acc_ref)
    live = count_ref[0, step]
    for q in range(rows_ref.shape[0]):

        @pl.when(q < live)
        def _():
            acc_ref[rows_ref[q, 0, step], cols_ref[q, 0, step]] += tile_at(q).astype(F32)

    dense = jnp.concatenate(
        [jnp.concatenate([acc_ref[row, col] for col in range(2)], axis=1) for row in range(2)],
        axis=0,
    ).astype(BF16)
    out_ref[...] = contract_rows(dense, own).astype(out_ref.dtype)


def first_kernel(yl_ref, *refs, odd, role):
    tiles_ref, *sources, out_ref, held_ref = refs[:8]
    *held, acc_ref, sems = refs[8:]
    step = step_of(odd, role, yl_ref[0], tiles_ref.shape[1] // 2 - 1)
    copies = [
        pltpu.make_async_copy(source, kept, sems.at[at])
        for at, (source, kept) in enumerate(
            [*zip(sources, held), (tiles_ref.at[0, step], held_ref)]
        )
    ]
    for copy in copies:
        copy.start()
    for copy in copies:
        copy.wait()
    rows_ref, cols_ref, count_ref, pre_ref, up_ref = held
    own = masked(pre_ref[...], up_ref[...])
    term(lambda q: held_ref[q], rows_ref, cols_ref, count_ref, step, own, out_ref, acc_ref)


def terms_kernel(yl_ref, rows_ref, cols_ref, count_ref, tiles_ref, pre_ref, up_ref, *refs, roles):
    *out_refs, mark_ref, acc_ref, own_ref = refs[len(refs) - len(roles) - 3 :]
    mark_ref[...] = jnp.zeros_like(mark_ref)
    own_ref[...] = masked(pre_ref[...], up_ref[...])
    last = tiles_ref.shape[1] // 2 - 1
    for (odd, role), out_ref in zip(roles, out_refs):
        step = step_of(odd, role, yl_ref[0], last)
        term(
            lambda q: tiles_ref[0, step, q],
            rows_ref,
            cols_ref,
            count_ref,
            step,
            own_ref[...],
            out_ref,
            acc_ref,
        )


def gather_kernel(keep_ref, first_ref, second_ref, out_ref):
    total = keep_ref[...] + first_ref[...].astype(F32) + second_ref[...].astype(F32)
    out_ref[...] = total.astype(BF16)


def near_kernel(yl_ref, other_ref, keep_ref, first_ref, second_ref, spread_ref, out_ref):
    quarter = out_ref.shape[2]
    total = keep_ref[...] + first_ref[...].astype(F32) + second_ref[...].astype(F32)
    for low, lane in ((total.astype(BF16), yl_ref[0]), (other_ref[...], 1 - yl_ref[0])):
        for q in range(REP):
            span = slice(q * quarter, (q + 1) * quarter)
            out_ref[YL * q + lane] = jnp.dot(
                low, spread_ref[:, span], preferred_element_type=F32
            ).astype(BF16)


def sides_kernel(in_ref, *out_refs):
    for r, out_ref in enumerate(out_refs):
        total = in_ref[YL * r].astype(F32)
        for side in range(1, YL):
            total += in_ref[YL * r + side].astype(F32)
        out_ref[...] = total.astype(BF16)


def sum_kernel(left_ref, right_ref, out_ref, *mark_refs):
    for mark_ref in mark_refs:
        mark_ref[...] = jnp.zeros_like(mark_ref)
    total = left_ref[...].astype(F32) + right_ref[...].astype(F32)
    out_ref[...] = total.astype(out_ref.dtype)


def weight_kernel(*refs, scale):
    *in_refs, feat_ref, p_ref, gw_ref, lines_ref = refs
    total = in_refs[0][...].astype(F32)
    for in_ref in in_refs[1:]:
        total += in_ref[...].astype(F32)
    high = total.astype(BF16)
    low = (total - high.astype(F32)).astype(BF16)
    p_ref[0], p_ref[1] = high, low
    gw = (contract_rows(high, feat_ref[...]) + contract_rows(low, feat_ref[...])) * scale
    quarter = lines_ref.shape[1]
    spots = ZH * ZL * YL
    rows, pieces = gw.shape[0] // spots, gw.shape[1] // quarter
    for i in range(rows):
        for f in range(pieces):
            lines_ref[pl.ds(f * rows + i, spots, rows * pieces), :] = gw[
                i * spots : (i + 1) * spots, f * quarter : (f + 1) * quarter
            ]
    gw_ref[...] = lines_ref[...].astype(BF16)


def pair_kernel(own_ref, other_ref, out_ref):
    out_ref[0] = own_ref[...]
    out_ref[1] = other_ref[...]


def feature_kernel(lane_ref, own_ref, other_ref, weight_ref, feat_ref):
    quarter = own_ref.shape[3]
    total = jnp.zeros(feat_ref.shape, F32)
    for at in range(REP):
        source = lane_ref[0] ^ at
        span = pl.ds(pl.multiple_of(source * quarter, quarter), quarter)
        for half in range(2):
            part = (own_ref if at < 2 else other_ref)[at % 2, half]
            total += jnp.dot(part, weight_ref[span, :], preferred_element_type=F32)
    feat_ref[...] = total.astype(BF16)


def copies_kernel(in_ref, out_ref):
    total = in_ref[0].astype(F32)
    for d in range(1, in_ref.shape[0]):
        total += in_ref[d].astype(F32)
    for r in range(out_ref.shape[0]):
        out_ref[r] = total


def lines_kernel(in_ref, gw_ref):
    lanes, lines, quarter = in_ref.shape
    pieces = gw_ref.shape[1] // quarter
    rows = lines // pieces
    for q in range(lanes):
        for f in range(pieces):
            gw_ref[q * rows : (q + 1) * rows, f * quarter : (f + 1) * quarter] = in_ref[
                q, f * rows : (f + 1) * rows, :
            ]


def whole(kernel, outs, scalars, arrays, scratch=(), space=pltpu.VMEM, limit=48):
    return pl.pallas_call(
        kernel,
        in_specs=[pl.BlockSpec(memory_space=pltpu.SMEM)] * len(scalars)
        + [pl.BlockSpec(memory_space=space)] * len(arrays),
        out_specs=jax.tree.map(lambda _: pl.BlockSpec(memory_space=pltpu.VMEM), outs),
        out_shape=outs,
        scratch_shapes=scratch,
        compiler_params=pltpu.CompilerParams(vmem_limit_bytes=limit * 1024 * 1024),
    )(*scalars, *arrays)


def exchange(value, axes):
    return lax.all_to_all(value, axes, 0, 0)


def along_z(value, shift):
    count = ZH * ZL
    return lax.ppermute(value, ("zh", "zl"), [(z, (z + shift) % count) for z in range(count)])


def turned_along_z(value, shift):
    count = ZH * ZL
    pairs = [
        (z * YL + y, (z + (shift if y else -shift)) % count * YL + y)
        for z in range(count)
        for y in range(YL)
    ]
    return lax.ppermute(value, BLK, pairs)


def shards(features, pre_act, upstream, weight, tile_values, tile_rows, tile_cols, tile_count):
    _, steps, slots, tile, _ = tile_values.shape
    nodes, width = features.shape
    hidden = upstream.shape[1]
    quarter = width // REP
    scale = float(nodes * ZH * ZL * YL) ** -0.5
    shape = jax.ShapeDtypeStruct

    lists = (tile_rows.transpose(2, 0, 1), tile_cols.transpose(2, 0, 1), tile_count)
    mark = shape((8, tile), F32)

    yl = lax.axis_index("yl").reshape(1)

    gates = (pre_act, upstream)
    block = shape((nodes, hidden), BF16)
    acc = pltpu.VMEM((2, 2, tile, tile), F32)

    def terms(roles, kinds, marks=()):
        return whole(
            functools.partial(terms_kernel, roles=roles),
            tuple(shape((nodes, hidden), kind) for kind in kinds) + (mark,),
            (yl, *lists),
            (tile_values, *gates, *marks),
            (acc, pltpu.VMEM(block.shape, block.dtype)),
        )

    far_other = whole(
        functools.partial(first_kernel, odd=1, role=0),
        (block,),
        (yl,),
        (tile_values, *lists, *gates),
        (
            pltpu.VMEM((slots, tile, tile), BF16),
            *(pltpu.SMEM(listed.shape, listed.dtype) for listed in lists),
            *(pltpu.VMEM(gate.shape, gate.dtype) for gate in gates),
            acc,
            pltpu.SemaphoreType.DMA((6,)),
        ),
        pltpu.HBM,
        60,
    )[0]
    far_same, back_other, mid_other, _ = terms(((0, 0), (1, 3), (1, 1)), (BF16, BF16, F32))
    mid_other, mark_other = whole(
        sum_kernel, (block, mark), (), (mid_other, turned_along_z(far_other, 1))
    )
    mid_same, back_same, mark_same = terms(((0, 1), (0, 3)), (F32, BF16), (mark_other,))
    keep_other, keep_same, _ = terms(((1, 2), (0, 2)), (F32, F32), (mark_same,))
    mid_same = whole(sum_kernel, (block,), (), (mid_same, along_z(far_same, 1)))[0]
    mid_other = turned_along_z(mid_other, 1)
    back_other = turned_along_z(back_other, -1)
    mid_same = along_z(mid_same, 1)
    back_same = along_z(back_same, -1)
    other = whole(gather_kernel, (block,), (), (keep_other, mid_other, back_other))[0]

    spread = np.zeros((hidden, hidden), np.float32)
    spread[hidden_order(hidden), np.arange(hidden)] = 1.0
    spread = jnp.asarray(spread, BF16)
    weight = contract_rows(spread, weight).astype(BF16)
    parts = whole(
        near_kernel,
        (shape((REP * YL, nodes, quarter), BF16),),
        (yl,),
        (other, keep_same, mid_same, back_same, spread),
    )[0]
    parts = exchange(parts, ("rep", "yl"))
    parts = whole(sides_kernel, (shape((nodes, quarter), BF16),) * REP, (), (parts,))
    hops = (-2, -6, 6, 2)
    parts = [along_z(parts[r], hops[r]) for r in range(REP)]
    far = whole(sum_kernel, (shape((nodes, quarter), F32),), (), (parts[1], parts[2]))[0]
    p_quarter, gw = whole(
        functools.partial(weight_kernel, scale=scale),
        (shape((2, nodes, quarter), BF16), shape((hidden, quarter), BF16)),
        (),
        (far, parts[0], parts[3], features),
        (pltpu.VMEM((hidden, quarter), F32),),
    )
    gw = exchange(gw.reshape(ZH * ZL * YL, -1, quarter), BLK)
    gw = whole(copies_kernel, (shape((REP,) + gw.shape[1:], F32),), (), (gw,))[0]
    gw = exchange(gw, "rep")
    lane = lax.axis_index("rep").reshape(1)
    other = lax.ppermute(p_quarter, "rep", [(r, r ^ 1) for r in range(REP)])
    pair = whole(pair_kernel, (shape((2, 2, nodes, quarter), BF16),), (), (p_quarter, other))[0]
    others = lax.ppermute(pair, "rep", [(r, r ^ 2) for r in range(REP)])
    grad_feat = whole(
        feature_kernel, (shape((nodes, width), BF16),), (lane,), (pair, others, weight)
    )[0]
    rows = hidden // (ZH * ZL * YL)
    grad_weight = whole(lines_kernel, (shape((rows, width), F32),), (), (gw,))[0]
    return grad_feat, grad_weight


def solution(mesh):
    dp = mesh.shape["dp"]
    fine = Mesh(mesh.devices.reshape(dp, REP, ZH, ZL, YL), ("dp", "rep") + BLK)
    rows = ("dp",) + BLK
    return jax.shard_map(
        shards,
        mesh=fine,
        in_specs=(
            P(rows, None),
            P(rows, None),
            P(rows, None),
            P(),
            P(rows, "rep", None, None, None),
            P(rows, "rep", None),
            P(rows, "rep", None),
            P(rows, "rep"),
        ),
        out_specs=(P(rows, None), P(rows, None)),
        check_vma=False,
    )
```

```python
import functools

import jax
import jax.numpy as jnp
import numpy as np
from jax import lax
from jax.experimental import pallas as pl
from jax.experimental.pallas import tpu as pltpu
from jax.sharding import Mesh, PartitionSpec as P

ZH, ZL, YL, REP = 4, 4, 2, 4
BLK = ("zh", "zl", "yl")
BF16, F32 = jnp.bfloat16, jnp.float32


def contract_rows(left, right):
    return lax.dot_general(left, right, (((0,), (0,)), ((), ())), preferred_element_type=F32)


def hidden_order(width):
    units = np.arange(width).reshape(ZH * ZL * YL, REP, -1)
    return units.transpose(1, 2, 0).reshape(-1)


def masked(pre_act, upstream):
    return jnp.where(pre_act > 0, upstream, jnp.zeros_like(upstream))


def step_of(odd, role, yl, last):
    return 2 * jnp.where(yl == 0, last - role, role) + 1 if odd else 2 * role


def term(tile_at, rows_ref, cols_ref, count_ref, step, own, out_ref, acc_ref):
    acc_ref[...] = jnp.zeros_like(acc_ref)
    live = count_ref[0, step]
    for q in range(rows_ref.shape[0]):

        @pl.when(q < live)
        def _():
            acc_ref[rows_ref[q, 0, step], cols_ref[q, 0, step]] += tile_at(q).astype(F32)

    dense = jnp.concatenate(
        [jnp.concatenate([acc_ref[row, col] for col in range(2)], axis=1) for row in range(2)],
        axis=0,
    ).astype(BF16)
    out_ref[...] = contract_rows(dense, own).astype(out_ref.dtype)


def first_kernel(yl_ref, *refs, odd, role):
    tiles_ref, *sources, out_ref, held_ref = refs[:8]
    *held, acc_ref, sems = refs[8:]
    step = step_of(odd, role, yl_ref[0], tiles_ref.shape[1] // 2 - 1)
    copies = [
        pltpu.make_async_copy(source, kept, sems.at[at])
        for at, (source, kept) in enumerate(
            [*zip(sources, held), (tiles_ref.at[0, step], held_ref)]
        )
    ]
    for copy in copies:
        copy.start()
    for copy in copies:
        copy.wait()
    rows_ref, cols_ref, count_ref, pre_ref, up_ref = held
    own = masked(pre_ref[...], up_ref[...])
    term(lambda q: held_ref[q], rows_ref, cols_ref, count_ref, step, own, out_ref, acc_ref)


def terms_kernel(yl_ref, rows_ref, cols_ref, count_ref, tiles_ref, pre_ref, up_ref, *refs, roles):
    *out_refs, mark_ref, acc_ref, own_ref = refs[len(refs) - len(roles) - 3 :]
    mark_ref[...] = jnp.zeros_like(mark_ref)
    own_ref[...] = masked(pre_ref[...], up_ref[...])
    last = tiles_ref.shape[1] // 2 - 1
    for (odd, role), out_ref in zip(roles, out_refs):
        step = step_of(odd, role, yl_ref[0], last)
        term(
            lambda q: tiles_ref[0, step, q],
            rows_ref,
            cols_ref,
            count_ref,
            step,
            own_ref[...],
            out_ref,
            acc_ref,
        )


def gather_kernel(keep_ref, first_ref, second_ref, out_ref):
    total = keep_ref[...] + first_ref[...].astype(F32) + second_ref[...].astype(F32)
    out_ref[...] = total.astype(BF16)


def near_kernel(yl_ref, other_ref, keep_ref, first_ref, second_ref, spread_ref, out_ref):
    quarter = out_ref.shape[2]
    total = keep_ref[...] + first_ref[...].astype(F32) + second_ref[...].astype(F32)
    for low, lane in ((total.astype(BF16), yl_ref[0]), (other_ref[...], 1 - yl_ref[0])):
        for q in range(REP):
            span = slice(q * quarter, (q + 1) * quarter)
            out_ref[YL * q + lane] = jnp.dot(
                low, spread_ref[:, span], preferred_element_type=F32
            ).astype(BF16)


def sides_kernel(in_ref, *out_refs):
    for r, out_ref in enumerate(out_refs):
        total = in_ref[YL * r].astype(F32)
        for side in range(1, YL):
            total += in_ref[YL * r + side].astype(F32)
        out_ref[...] = total.astype(out_ref.dtype)


def sum_kernel(left_ref, right_ref, out_ref, *mark_refs):
    for mark_ref in mark_refs:
        mark_ref[...] = jnp.zeros_like(mark_ref)
    total = left_ref[...].astype(F32) + right_ref[...].astype(F32)
    out_ref[...] = total.astype(out_ref.dtype)


def weight_kernel(*refs, scale):
    *in_refs, feat_ref, p_ref, gw_ref, lines_ref = refs
    total = in_refs[0][...].astype(F32)
    for in_ref in in_refs[1:]:
        total += in_ref[...].astype(F32)
    high = total.astype(BF16)
    low = (total - high.astype(F32)).astype(BF16)
    p_ref[0], p_ref[1] = high, low
    gw = (contract_rows(high, feat_ref[...]) + contract_rows(low, feat_ref[...])) * scale
    quarter = lines_ref.shape[1]
    spots = ZH * ZL * YL
    rows, pieces = gw.shape[0] // spots, gw.shape[1] // quarter
    for i in range(rows):
        for f in range(pieces):
            lines_ref[pl.ds(f * rows + i, spots, rows * pieces), :] = gw[
                i * spots : (i + 1) * spots, f * quarter : (f + 1) * quarter
            ]
    gw_ref[...] = lines_ref[...].astype(BF16)


def feature_kernel(lane_ref, *refs):
    *in_refs, weight_ref, feat_ref = refs
    quarter = in_refs[0].shape[2]
    total = jnp.zeros(feat_ref.shape, F32)
    for back, in_ref in enumerate(in_refs):
        source = lax.rem(lane_ref[0] + REP - back, REP)
        span = pl.ds(pl.multiple_of(source * quarter, quarter), quarter)
        for half in range(2):
            total += jnp.dot(in_ref[half], weight_ref[span, :], preferred_element_type=F32)
    feat_ref[...] = total.astype(BF16)


def copies_kernel(in_ref, out_ref):
    total = in_ref[0].astype(F32)
    for d in range(1, in_ref.shape[0]):
        total += in_ref[d].astype(F32)
    for r in range(out_ref.shape[0]):
        out_ref[r] = total


def lines_kernel(in_ref, gw_ref):
    lanes, lines, quarter = in_ref.shape
    pieces = gw_ref.shape[1] // quarter
    rows = lines // pieces
    for q in range(lanes):
        for f in range(pieces):
            gw_ref[q * rows : (q + 1) * rows, f * quarter : (f + 1) * quarter] = in_ref[
                q, f * rows : (f + 1) * rows, :
            ]


def whole(kernel, outs, scalars, arrays, scratch=(), space=pltpu.VMEM, limit=48):
    return pl.pallas_call(
        kernel,
        in_specs=[pl.BlockSpec(memory_space=pltpu.SMEM)] * len(scalars)
        + [pl.BlockSpec(memory_space=space)] * len(arrays),
        out_specs=jax.tree.map(lambda _: pl.BlockSpec(memory_space=pltpu.VMEM), outs),
        out_shape=outs,
        scratch_shapes=scratch,
        compiler_params=pltpu.CompilerParams(vmem_limit_bytes=limit * 1024 * 1024),
    )(*scalars, *arrays)


def exchange(value, axes):
    return lax.all_to_all(value, axes, 0, 0)


def along_z(value, shift):
    count = ZH * ZL
    return lax.ppermute(value, ("zh", "zl"), [(z, (z + shift) % count) for z in range(count)])


def turned_along_z(value, shift):
    count = ZH * ZL
    pairs = [
        (z * YL + y, (z + (shift if y else -shift)) % count * YL + y)
        for z in range(count)
        for y in range(YL)
    ]
    return lax.ppermute(value, BLK, pairs)


def shards(features, pre_act, upstream, weight, tile_values, tile_rows, tile_cols, tile_count):
    _, steps, slots, tile, _ = tile_values.shape
    nodes, width = features.shape
    hidden = upstream.shape[1]
    quarter = width // REP
    scale = float(nodes * ZH * ZL * YL) ** -0.5
    shape = jax.ShapeDtypeStruct

    lists = (tile_rows.transpose(2, 0, 1), tile_cols.transpose(2, 0, 1), tile_count)
    mark = shape((8, tile), F32)

    yl = lax.axis_index("yl").reshape(1)

    gates = (pre_act, upstream)
    block = shape((nodes, hidden), BF16)
    acc = pltpu.VMEM((2, 2, tile, tile), F32)

    def terms(roles, kinds, marks=()):
        return whole(
            functools.partial(terms_kernel, roles=roles),
            tuple(shape((nodes, hidden), kind) for kind in kinds) + (mark,),
            (yl, *lists),
            (tile_values, *gates, *marks),
            (acc, pltpu.VMEM(block.shape, block.dtype)),
        )

    far_other = whole(
        functools.partial(first_kernel, odd=1, role=0),
        (block,),
        (yl,),
        (tile_values, *lists, *gates),
        (
            pltpu.VMEM((slots, tile, tile), BF16),
            *(pltpu.SMEM(listed.shape, listed.dtype) for listed in lists),
            *(pltpu.VMEM(gate.shape, gate.dtype) for gate in gates),
            acc,
            pltpu.SemaphoreType.DMA((6,)),
        ),
        pltpu.HBM,
        60,
    )[0]
    far_same, back_other, mid_other, _ = terms(((0, 0), (1, 3), (1, 1)), (BF16, BF16, F32))
    mid_other, mark_other = whole(
        sum_kernel, (block, mark), (), (mid_other, turned_along_z(far_other, 1))
    )
    mid_same, back_same, mark_same = terms(((0, 1), (0, 3)), (F32, BF16), (mark_other,))
    keep_other, keep_same, _ = terms(((1, 2), (0, 2)), (F32, F32), (mark_same,))
    mid_same = whole(sum_kernel, (block,), (), (mid_same, along_z(far_same, 1)))[0]
    mid_other = turned_along_z(mid_other, 1)
    back_other = turned_along_z(back_other, -1)
    mid_same = along_z(mid_same, 1)
    back_same = along_z(back_same, -1)
    other = whole(gather_kernel, (block,), (), (keep_other, mid_other, back_other))[0]

    spread = np.zeros((hidden, hidden), np.float32)
    spread[hidden_order(hidden), np.arange(hidden)] = 1.0
    spread = jnp.asarray(spread, BF16)
    weight = contract_rows(spread, weight).astype(BF16)
    parts = whole(
        near_kernel,
        (shape((REP * YL, nodes, quarter), BF16),),
        (yl,),
        (other, keep_same, mid_same, back_same, spread),
    )[0]
    parts = exchange(parts, ("rep", "yl"))
    piece = shape((nodes, quarter), BF16)
    kept = shape((nodes, quarter), F32)
    down, down_far, up_far, up = whole(sides_kernel, (kept, piece, piece, kept), (), (parts,))
    down = whole(sum_kernel, (piece,), (), (down, along_z(down_far, -4)))[0]
    up = whole(sum_kernel, (piece,), (), (up, along_z(up_far, 4)))[0]
    down, up = along_z(down, -2), along_z(up, 2)
    p_quarter, gw = whole(
        functools.partial(weight_kernel, scale=scale),
        (shape((2, nodes, quarter), BF16), shape((hidden, quarter), BF16)),
        (),
        (down, up, features),
        (pltpu.VMEM((hidden, quarter), F32),),
    )
    gw = exchange(gw.reshape(ZH * ZL * YL, -1, quarter), BLK)
    gw = whole(copies_kernel, (shape((REP,) + gw.shape[1:], F32),), (), (gw,))[0]
    gw = exchange(gw, "rep")
    lane = lax.axis_index("rep").reshape(1)
    p_all = [p_quarter] + [
        lax.ppermute(p_quarter, "rep", [(r, (r + back) % REP) for r in range(REP)])
        for back in range(1, REP)
    ]
    grad_feat = whole(
        feature_kernel, (shape((nodes, width), BF16),), (lane,), (*p_all, weight)
    )[0]
    rows = hidden // (ZH * ZL * YL)
    grad_weight = whole(lines_kernel, (shape((rows, width), F32),), (), (gw,))[0]
    return grad_feat, grad_weight


def solution(mesh):
    dp = mesh.shape["dp"]
    fine = Mesh(mesh.devices.reshape(dp, REP, ZH, ZL, YL), ("dp", "rep") + BLK)
    rows = ("dp",) + BLK
    return jax.shard_map(
        shards,
        mesh=fine,
        in_specs=(
            P(rows, None),
            P(rows, None),
            P(rows, None),
            P(),
            P(rows, "rep", None, None, None),
            P(rows, "rep", None),
            P(rows, "rep", None),
            P(rows, "rep"),
        ),
        out_specs=(P(rows, None), P(rows, None)),
        check_vma=False,
    )
```

```python
import functools

import jax
import jax.numpy as jnp
import numpy as np
from jax import lax
from jax.experimental import pallas as pl
from jax.experimental.pallas import tpu as pltpu
from jax.sharding import Mesh, PartitionSpec as P

ZH, ZL, YL, REP = 4, 4, 2, 4
BLK = ("zh", "zl", "yl")
BF16, F32 = jnp.bfloat16, jnp.float32


def contract_rows(left, right):
    return lax.dot_general(left, right, (((0,), (0,)), ((), ())), preferred_element_type=F32)


def hidden_order(width):
    units = np.arange(width).reshape(ZH * ZL * YL, REP, -1)
    return units.transpose(1, 2, 0).reshape(-1)


def masked(pre_act, upstream):
    return jnp.where(pre_act > 0, upstream, jnp.zeros_like(upstream))


def step_of(odd, role, yl, last):
    return 2 * jnp.where(yl == 0, last - role, role) + 1 if odd else 2 * role


def term(tile_at, rows_ref, cols_ref, count_ref, step, own, out_ref, acc_ref):
    acc_ref[...] = jnp.zeros_like(acc_ref)
    live = count_ref[0, step]
    for q in range(rows_ref.shape[0]):

        @pl.when(q < live)
        def _():
            acc_ref[rows_ref[q, 0, step], cols_ref[q, 0, step]] += tile_at(q).astype(F32)

    dense = jnp.concatenate(
        [jnp.concatenate([acc_ref[row, col] for col in range(2)], axis=1) for row in range(2)],
        axis=0,
    ).astype(BF16)
    out_ref[...] = contract_rows(dense, own).astype(out_ref.dtype)


def first_kernel(yl_ref, *refs, odd, role):
    tiles_ref, *sources, out_ref, held_ref = refs[:8]
    *held, acc_ref, sems = refs[8:]
    step = step_of(odd, role, yl_ref[0], tiles_ref.shape[1] // 2 - 1)
    copies = [
        pltpu.make_async_copy(source, kept, sems.at[at])
        for at, (source, kept) in enumerate(
            [*zip(sources, held), (tiles_ref.at[0, step], held_ref)]
        )
    ]
    for copy in copies:
        copy.start()
    for copy in copies:
        copy.wait()
    rows_ref, cols_ref, count_ref, pre_ref, up_ref = held
    own = masked(pre_ref[...], up_ref[...])
    term(lambda q: held_ref[q], rows_ref, cols_ref, count_ref, step, own, out_ref, acc_ref)


def terms_kernel(yl_ref, rows_ref, cols_ref, count_ref, tiles_ref, pre_ref, up_ref, *refs, roles):
    *out_refs, mark_ref, acc_ref, own_ref = refs[len(refs) - len(roles) - 3 :]
    mark_ref[...] = jnp.zeros_like(mark_ref)
    own_ref[...] = masked(pre_ref[...], up_ref[...])
    last = tiles_ref.shape[1] // 2 - 1
    for (odd, role), out_ref in zip(roles, out_refs):
        step = step_of(odd, role, yl_ref[0], last)
        term(
            lambda q: tiles_ref[0, step, q],
            rows_ref,
            cols_ref,
            count_ref,
            step,
            own_ref[...],
            out_ref,
            acc_ref,
        )


def by_quarters(total, spread_ref):
    low = total.astype(BF16)
    quarter = low.shape[1] // REP
    for q in range(REP):
        span = slice(q * quarter, (q + 1) * quarter)
        yield q, jnp.dot(low, spread_ref[:, span], preferred_element_type=F32).astype(BF16)


def gather_kernel(keep_ref, first_ref, second_ref, spread_ref, out_ref):
    total = keep_ref[...] + first_ref[...].astype(F32) + second_ref[...].astype(F32)
    for q, piece in by_quarters(total, spread_ref):
        out_ref[q] = piece


def near_kernel(yl_ref, other_ref, keep_ref, first_ref, second_ref, spread_ref, out_ref):
    total = keep_ref[...] + first_ref[...].astype(F32) + second_ref[...].astype(F32)
    for q, piece in by_quarters(total, spread_ref):
        out_ref[YL * q + yl_ref[0]] = piece
        out_ref[YL * q + 1 - yl_ref[0]] = other_ref[q]


def sides_kernel(in_ref, *out_refs):
    for r, out_ref in enumerate(out_refs):
        total = in_ref[YL * r].astype(F32)
        for side in range(1, YL):
            total += in_ref[YL * r + side].astype(F32)
        out_ref[...] = total.astype(out_ref.dtype)


def sum_kernel(left_ref, right_ref, out_ref, *mark_refs):
    for mark_ref in mark_refs:
        mark_ref[...] = jnp.zeros_like(mark_ref)
    total = left_ref[...].astype(F32) + right_ref[...].astype(F32)
    out_ref[...] = total.astype(out_ref.dtype)


def weight_kernel(*refs, scale):
    *in_refs, feat_ref, p_ref, gw_ref, lines_ref = refs
    total = in_refs[0][...].astype(F32)
    for in_ref in in_refs[1:]:
        total += in_ref[...].astype(F32)
    high = total.astype(BF16)
    low = (total - high.astype(F32)).astype(BF16)
    p_ref[0], p_ref[1] = high, low
    gw = (contract_rows(high, feat_ref[...]) + contract_rows(low, feat_ref[...])) * scale
    quarter = lines_ref.shape[1]
    spots = ZH * ZL * YL
    rows, pieces = gw.shape[0] // spots, gw.shape[1] // quarter
    for i in range(rows):
        for f in range(pieces):
            lines_ref[pl.ds(f * rows + i, spots, rows * pieces), :] = gw[
                i * spots : (i + 1) * spots, f * quarter : (f + 1) * quarter
            ]
    gw_ref[...] = lines_ref[...].astype(BF16)


def feature_kernel(lane_ref, *refs):
    *in_refs, weight_ref, feat_ref = refs
    quarter = in_refs[0].shape[2]
    total = jnp.zeros(feat_ref.shape, F32)
    for back, in_ref in enumerate(in_refs):
        source = lax.rem(lane_ref[0] + REP - back, REP)
        span = pl.ds(pl.multiple_of(source * quarter, quarter), quarter)
        for half in range(2):
            total += jnp.dot(in_ref[half], weight_ref[span, :], preferred_element_type=F32)
    feat_ref[...] = total.astype(BF16)


def copies_kernel(in_ref, out_ref):
    total = in_ref[0].astype(F32)
    for d in range(1, in_ref.shape[0]):
        total += in_ref[d].astype(F32)
    for r in range(out_ref.shape[0]):
        out_ref[r] = total


def lines_kernel(in_ref, gw_ref):
    lanes, lines, quarter = in_ref.shape
    pieces = gw_ref.shape[1] // quarter
    rows = lines // pieces
    for q in range(lanes):
        for f in range(pieces):
            gw_ref[q * rows : (q + 1) * rows, f * quarter : (f + 1) * quarter] = in_ref[
                q, f * rows : (f + 1) * rows, :
            ]


def whole(kernel, outs, scalars, arrays, scratch=(), space=pltpu.VMEM, limit=48):
    return pl.pallas_call(
        kernel,
        in_specs=[pl.BlockSpec(memory_space=pltpu.SMEM)] * len(scalars)
        + [pl.BlockSpec(memory_space=space)] * len(arrays),
        out_specs=jax.tree.map(lambda _: pl.BlockSpec(memory_space=pltpu.VMEM), outs),
        out_shape=outs,
        scratch_shapes=scratch,
        compiler_params=pltpu.CompilerParams(vmem_limit_bytes=limit * 1024 * 1024),
    )(*scalars, *arrays)


def exchange(value, axes):
    return lax.all_to_all(value, axes, 0, 0)


def along_z(value, shift):
    count = ZH * ZL
    return lax.ppermute(value, ("zh", "zl"), [(z, (z + shift) % count) for z in range(count)])


def turned_along_z(value, shift):
    count = ZH * ZL
    pairs = [
        (z * YL + y, (z + (shift if y else -shift)) % count * YL + y)
        for z in range(count)
        for y in range(YL)
    ]
    return lax.ppermute(value, BLK, pairs)


def shards(features, pre_act, upstream, weight, tile_values, tile_rows, tile_cols, tile_count):
    _, steps, slots, tile, _ = tile_values.shape
    nodes, width = features.shape
    hidden = upstream.shape[1]
    quarter = width // REP
    scale = float(nodes * ZH * ZL * YL) ** -0.5
    shape = jax.ShapeDtypeStruct

    lists = (tile_rows.transpose(2, 0, 1), tile_cols.transpose(2, 0, 1), tile_count)
    mark = shape((8, tile), F32)

    yl = lax.axis_index("yl").reshape(1)

    gates = (pre_act, upstream)
    block = shape((nodes, hidden), BF16)
    acc = pltpu.VMEM((2, 2, tile, tile), F32)

    def terms(roles, kinds, marks=()):
        return whole(
            functools.partial(terms_kernel, roles=roles),
            tuple(shape((nodes, hidden), kind) for kind in kinds) + (mark,),
            (yl, *lists),
            (tile_values, *gates, *marks),
            (acc, pltpu.VMEM(block.shape, block.dtype)),
        )

    far_other = whole(
        functools.partial(first_kernel, odd=1, role=0),
        (block,),
        (yl,),
        (tile_values, *lists, *gates),
        (
            pltpu.VMEM((slots, tile, tile), BF16),
            *(pltpu.SMEM(listed.shape, listed.dtype) for listed in lists),
            *(pltpu.VMEM(gate.shape, gate.dtype) for gate in gates),
            acc,
            pltpu.SemaphoreType.DMA((6,)),
        ),
        pltpu.HBM,
        60,
    )[0]
    far_same, back_other, mid_other, _ = terms(((0, 0), (1, 3), (1, 1)), (BF16, BF16, F32))
    mid_other, mark_other = whole(
        sum_kernel, (block, mark), (), (mid_other, turned_along_z(far_other, 1))
    )
    mid_same, back_same, mark_same = terms(((0, 1), (0, 3)), (F32, BF16), (mark_other,))
    keep_other, keep_same, _ = terms(((1, 2), (0, 2)), (F32, F32), (mark_same,))
    mid_same = whole(sum_kernel, (block,), (), (mid_same, along_z(far_same, 1)))[0]
    mid_other = turned_along_z(mid_other, 1)
    back_other = turned_along_z(back_other, -1)
    mid_same = along_z(mid_same, 1)
    back_same = along_z(back_same, -1)

    spread = np.zeros((hidden, hidden), np.float32)
    spread[hidden_order(hidden), np.arange(hidden)] = 1.0
    spread = jnp.asarray(spread, BF16)
    other = whole(
        gather_kernel,
        (shape((REP, nodes, quarter), BF16),),
        (),
        (keep_other, mid_other, back_other, spread),
    )[0]
    weight = contract_rows(spread, weight).astype(BF16)
    parts = whole(
        near_kernel,
        (shape((REP * YL, nodes, quarter), BF16),),
        (yl,),
        (other, keep_same, mid_same, back_same, spread),
    )[0]
    parts = exchange(parts, ("rep", "yl"))
    piece = shape((nodes, quarter), BF16)
    kept = shape((nodes, quarter), F32)
    down, down_far, up_far, up = whole(sides_kernel, (kept, piece, piece, kept), (), (parts,))
    down = whole(sum_kernel, (piece,), (), (down, along_z(down_far, -4)))[0]
    up = whole(sum_kernel, (piece,), (), (up, along_z(up_far, 4)))[0]
    down, up = along_z(down, -2), along_z(up, 2)
    p_quarter, gw = whole(
        functools.partial(weight_kernel, scale=scale),
        (shape((2, nodes, quarter), BF16), shape((hidden, quarter), BF16)),
        (),
        (down, up, features),
        (pltpu.VMEM((hidden, quarter), F32),),
    )
    gw = exchange(gw.reshape(ZH * ZL * YL, -1, quarter), BLK)
    gw = whole(copies_kernel, (shape((REP,) + gw.shape[1:], F32),), (), (gw,))[0]
    gw = exchange(gw, "rep")
    lane = lax.axis_index("rep").reshape(1)
    p_all = [p_quarter] + [
        lax.ppermute(p_quarter, "rep", [(r, (r + back) % REP) for r in range(REP)])
        for back in range(1, REP)
    ]
    grad_feat = whole(
        feature_kernel, (shape((nodes, width), BF16),), (lane,), (*p_all, weight)
    )[0]
    rows = hidden // (ZH * ZL * YL)
    grad_weight = whole(lines_kernel, (shape((rows, width), F32),), (), (gw,))[0]
    return grad_feat, grad_weight


def solution(mesh):
    dp = mesh.shape["dp"]
    fine = Mesh(mesh.devices.reshape(dp, REP, ZH, ZL, YL), ("dp", "rep") + BLK)
    rows = ("dp",) + BLK
    return jax.shard_map(
        shards,
        mesh=fine,
        in_specs=(
            P(rows, None),
            P(rows, None),
            P(rows, None),
            P(),
            P(rows, "rep", None, None, None),
            P(rows, "rep", None),
            P(rows, "rep", None),
            P(rows, "rep"),
        ),
        out_specs=(P(rows, None), P(rows, None)),
        check_vma=False,
    )
```
